256 devices in a mesh: patch: 32 (over y_lo, z, core), tensor: 8 (over y_hi, x).
Axes of the slice: x: 4, y: 4 (y_hi: 2, y_lo: 2; y = y_hi * 2 + y_lo), z: 8, core: 2. Of those that a mesh axis runs over, the one named last changes fastest.
Arguments:
- tokens: bfloat16 [8192, 3072], P('patch', 'tensor'), may hold values from -6 to 6
- shift: float32 [3072], replicated, may hold values from -3 to 3
- scale: float32 [3072], replicated, may hold values from -0.9 to 0.9
- gate: float32 [3072], P('tensor'), may hold values from 0.5 to 1.5
- w_qkv: bfloat16 [3072, 3, 3072], P(None, None, 'tensor'), may hold values from -0.109375 to 0.109375
- w_out: bfloat16 [3072, 3072], P('tensor'), may hold values from -0.109375 to 0.109375
- stale_keys: bfloat16 [8192, 3072], P('patch', 'tensor'), may hold values from -180 to 180
- stale_values: bfloat16 [8192, 3072], P('patch', 'tensor'), may hold values from -6 to 6
Outputs:
- mixed: bfloat16 [8192, 3072], P('patch', 'tensor')
- branch: float32 [8192, 3072], P('patch', 'tensor')
The draws below stay inside these ranges and needn't reach their ends.
All inputs are finite; a program needn't handle non-finite values.
Results may differ from the reference program's by a relative error of at most 0.017.
The reference program's roundings to bfloat16 on the way count: a program that leaves them out, or rounds other values in their place, can miss the bound.
Values may be sent and summed in bfloat16 or wider, within the bound.
A program may use at most 128 MiB of HBM per device.

```python
import jax
import jax.numpy as jnp
from jax import lax

D = 3072
HEADS = 24
HD = 128
TOK_DEV = 256
TOKENS = 8192
N_PATCH = 32


def draw_stale_keys(key, part):
    key = jax.random.fold_in(key, 11)
    base_key = jax.random.fold_in(key, 0)
    base = jnp.clip(jax.random.normal(base_key, (TOKENS, HEADS * HD), jnp.float32), -6.0, 6.0)
    return base.astype(jnp.bfloat16)


def level_of(stream_key, extent, shards, low, largest):
    level, own = 1.0, jax.random.fold_in(stream_key, 6)
    for position, parts in shards:
        heights = jnp.exp(jax.random.uniform(jax.random.fold_in(own, position), (parts,), jnp.float32, low / len(shards), largest / len(shards)))
        level = level * jnp.repeat(heights, extent[position] // parts).reshape([-1 if axis == position else 1 for axis in range(len(extent))])
    return level


def normal_values(own_key, dims, scale, bound, cuts=(), kind=jnp.bfloat16):
    factor_of = level_of(own_key, dims, cuts, -0.22, 0.18) if cuts else 1.0
    result = jax.random.normal(own_key, dims, jnp.float32) * scale * factor_of
    return jnp.minimum(jnp.maximum(result, -bound), bound).astype(kind)


def setup_inputs(seed: int = 0) -> dict:
    keys = jax.random.split(jax.random.key(seed), 9)
    return {
        "tokens": normal_values(keys[0], (TOKENS, D), 1.0, 6.0, ((0, 32), (1, 8))),
        "shift": normal_values(keys[1], (D,), 0.5, 3.0, (), jnp.float32),
        "scale": normal_values(keys[2], (D,), 0.3, 0.9, (), jnp.float32),
        "gate": jnp.clip(0.5 + 1.0 * jax.random.uniform(keys[3], (D,), jnp.float32) ** level_of(keys[3], (D,), ((0, 8),), -0.2, 0.2), 0.5, 1.5),
        "w_qkv": normal_values(keys[4], (D, 3, HEADS * HD), D ** -0.5, 0.109375, ((2, 8),)),
        "w_out": normal_values(keys[5], (HEADS * HD, D), (HEADS * HD) ** -0.5, 0.109375, ((0, 8),)),
        "stale_keys": draw_stale_keys(jax.random.fold_in(keys[8], 71), 0),
        "stale_values": normal_values(keys[7], (TOKENS, HEADS * HD), 1.0, 6.0, ((0, 32), (1, 8))),
    }


def reference(tokens, shift, scale, gate, w_qkv, w_out, stale_keys, stale_values):
    inputs = tokens.astype(jnp.float32)
    center = lax.optimization_barrier(jnp.mean(inputs, axis=1, keepdims=True))
    spread = lax.optimization_barrier(jnp.mean((inputs - center) ** 2, axis=1, keepdims=True))
    normed = (inputs - center) * lax.rsqrt(spread + 1e-06)
    modulated = (normed * (1.0 + scale) + shift).astype(jnp.bfloat16)
    width = HEADS * HD
    qkv = jnp.dot(modulated, w_qkv.reshape(D, 3 * width), preferred_element_type=jnp.float32).astype(jnp.bfloat16)

    def by_head(matrix):
        return matrix.reshape(TOKENS, HEADS, HD).transpose(1, 0, 2)
    query = by_head(qkv[:, :width])
    fresh_keys = by_head(qkv[:, width:2 * width])
    fresh_values = by_head(qkv[:, 2 * width:])
    old_keys = by_head(stale_keys)
    old_values = by_head(stale_values)
    own_block = jnp.eye(N_PATCH, dtype=bool)[:, None, :, None]
    inv_root = 1.0 / jnp.sqrt(jnp.float32(HD))

    def one_head(operands):
        head_query, head_keys, head_values, head_old_keys, head_old_values = operands
        blocks_query = head_query.astype(jnp.float32).reshape(N_PATCH, TOK_DEV, HD)
        blocks_keys = head_keys.astype(jnp.float32).reshape(N_PATCH, TOK_DEV, HD)
        blocks_values = head_values.astype(jnp.float32).reshape(N_PATCH, TOK_DEV, HD)
        older_keys = head_old_keys.astype(jnp.float32).reshape(N_PATCH, TOK_DEV, HD)
        older_values = head_old_values.astype(jnp.float32).reshape(N_PATCH, TOK_DEV, HD)
        stale_score = jnp.einsum('ptd,qud->ptqu', blocks_query, older_keys) * inv_root
        fresh_score = jnp.einsum('ptd,pud->ptu', blocks_query, blocks_keys) * inv_root
        score = jnp.where(own_block, fresh_score[:, :, None, :], stale_score)
        highest = lax.optimization_barrier(jnp.max(score, axis=(2, 3), keepdims=True))
        expo = jnp.exp(score - highest)
        total = lax.optimization_barrier(jnp.sum(expo, axis=(2, 3)))
        rounded = lax.optimization_barrier(expo.astype(jnp.bfloat16)).astype(jnp.float32)
        remote = jnp.where(own_block, 0.0, rounded)
        local_part = lax.optimization_barrier(jnp.sum(jnp.where(own_block, rounded, 0.0), axis=2))
        accum = jnp.einsum('ptqu,qud->ptd', remote, older_values) + jnp.einsum('ptu,pud->ptd', local_part, blocks_values)
        return (accum / total[:, :, None]).astype(jnp.bfloat16).reshape(TOKENS, HD)
    attended = lax.map(one_head, (query, fresh_keys, fresh_values, old_keys, old_values))
    attended = attended.transpose(1, 0, 2).reshape(TOKENS, width)
    projected = jnp.dot(attended, w_out, preferred_element_type=jnp.float32)
    branch = gate * projected
    return ((inputs + branch).astype(jnp.bfloat16), branch)
```

```python
import jax
import jax.numpy as jnp
from jax import lax
from jax.experimental import pallas as pl
from jax.experimental.pallas import tpu as pltpu
from jax.sharding import PartitionSpec as P

MESH = pl.DeviceIdType.MESH
HD = 128
ROWS = 256
NH = 3
WIDTH = NH * HD
D = 3072
NT = 8
NZ = 8
LOG2E = 1.4426950408889634
EXP_SCALE = LOG2E / (HD**0.5)
DEPTH = (4, 3)
F32 = jnp.float32
BF16 = jnp.bfloat16


def dot(a, b):
    return jnp.dot(a, b, preferred_element_type=F32)


def dot_t(a, b):
    return lax.dot_general(a, b, (((0,), (0,)), ((), ())), preferred_element_type=F32)


def kernel(
    tok_in, scale_ref, shift_ref, w_in, wo_in, sk_in, sv_in,
    out_ref,
    kv, tok, mod, w, wo, att, qown, qpart, qt, fresh, m_s, l_s, acc, mean_s, dev_s,
    osend, orecv, ssend, srecv,
    loc_sem, w_sem, ring_ss, ring_rs, d2d_ss, d2d_rs, tok_ss, tok_rs, att_ss, att_rs,
    q_ss, q_rs, o_ss, o_rs, st_ss, st_rs, wo_ss, wo_rs, wx_ss, wx_rs,
):
    p, t = lax.axis_index("patch"), lax.axis_index("tensor")
    b, z, c = lax.div(p, 16), lax.rem(lax.div(p, 2), NZ), lax.rem(p, 2)
    yh, x = lax.div(t, 4), lax.rem(t, 4)

    def dev(b=b, z=z, c=c, yh=yh, x=x):
        return (b * 16 + z * 2 + c, yh * 4 + x)

    def remote(src, dst, ss, rs, to):
        return pltpu.make_async_remote_copy(
            src_ref=src, dst_ref=dst, send_sem=ss, recv_sem=rs, device_id=to, device_id_type=MESH
        )

    dz = (1 - 2 * c, 2 * c - 1)
    zs = tuple(lax.rem(z + s + NZ, NZ) for s in dz)
    sibling, partner = dev(c=1 - c), dev(b=1 - b)
    xr, xl = dev(x=lax.rem(x + 1, 4)), dev(x=lax.rem(x + 3, 4))
    yo = dev(yh=1 - yh)
    me = z * 2 + c
    qtr = b * 2 + c

    loads = [pltpu.make_async_copy(tok_in, tok.at[t], loc_sem.at[0])]
    for h in range(NH):
        cols = pl.ds(h * HD, HD)
        loads.append(pltpu.make_async_copy(sk_in.at[:, cols], kv.at[me, h, 0], loc_sem.at[1 + 2 * h]))
        loads.append(pltpu.make_async_copy(sv_in.at[:, cols], kv.at[me, h, 1], loc_sem.at[2 + 2 * h]))
    own_cols = pl.ds(pl.multiple_of(t * WIDTH, WIDTH), WIDTH)
    wo_own = pltpu.make_async_copy(wo_in.at[:, qtr, :, own_cols], wo.at[t, :, qtr], loc_sem.at[7])
    w_loads = [pltpu.make_async_copy(w_in.at[j], w.at[j], w_sem.at[j]) for j in range(3)]
    for copy in loads + w_loads + [wo_own]:
        copy.start()

    barrier = pltpu.get_barrier_semaphore()
    peers = [sibling, partner, dev(z=zs[0]), dev(z=zs[1])]
    for e in range(1, NT):
        peers.append((p, lax.rem(t + e, NT)))
    for peer in peers:
        pl.semaphore_signal(barrier, inc=1, device_id=peer, device_id_type=MESH)
    pl.semaphore_wait(barrier, len(peers))

    sent = []

    def go(make, *args):
        make(*args).start()
        sent.append((make, args))

    def slot_of(s, d):
        return lax.rem(z - d * dz[s] + NZ, NZ) * 2 + c

    def ring(s, h, d):
        slot = slot_of(s, d)
        return remote(kv.at[slot, h], kv.at[slot, h], ring_ss.at[s, h, d], ring_rs.at[s, h, d], dev(z=zs[s]))

    def share(k, h, slot):
        return remote(kv.at[slot, h], kv.at[slot, h], d2d_ss.at[k, h], d2d_rs.at[k, h], sibling)

    def own_kv(h):
        loads[1 + 2 * h].wait()
        loads[2 + 2 * h].wait()
        go(ring, 0, h, 0)
        go(ring, 1, h, 0)
        go(share, 0, h, me)

    def event(h, d):
        for s in (0, 1):
            if d > DEPTH[s]:
                continue
            slot = slot_of(s, d)
            remote(
                kv.at[slot, h], kv.at[slot, h], ring_ss.at[s, h, d - 1], ring_rs.at[s, h, d - 1], sibling
            ).wait_recv()
            if d < DEPTH[s]:
                go(ring, s, h, d)
            go(lambda s=s: share(d + 4 * s, h, slot_of(s, d)))

    slot_l, slot_r, slot_f = (yh * 4 + lax.rem(x + e, 4) for e in (3, 1, 2))
    slot_y, slot_yl, slot_yr, slot_yf = ((1 - yh) * 4 + lax.rem(x + e, 4) for e in (0, 3, 1, 2))
    upper, lower = pl.ds(0, ROWS // 2), pl.ds(ROWS // 2, ROWS // 2)

    class Gather:
        def __init__(self, buf, ss, rs):
            self.buf, self.ss, self.rs = buf, ss, rs

        def view(self, slot, rows):
            return self.buf.at[slot] if rows is None else self.buf.at[slot, rows]

        def send(self, slot, rows, to, i, j):
            go(self.copy, slot, rows, to, i, j)

        def copy(self, slot, rows, to, i, j):
            view = self.view(slot, rows)
            return remote(view, view, self.ss.at[i], self.rs.at[j], to)

        def wait(self, slot, rows, j):
            view = self.view(slot, rows)
            remote(view, view, self.ss.at[0], self.rs.at[j], sibling).wait_recv()

        def start(self):
            self.send(t, None, yo, 2, 2)
            self.send(t, None, xr, 0, 0)
            self.send(t, None, xl, 1, 1)

        def near(self):
            self.wait(slot_l, None, 0)
            self.send(slot_l, upper, xr, 3, 5)
            self.wait(slot_r, None, 1)
            self.send(slot_r, lower, xl, 4, 6)

        def across(self):
            self.wait(slot_y, None, 2)
            self.send(slot_y, None, xr, 5, 3)
            self.send(slot_y, None, xl, 6, 4)

        def far(self):
            self.wait(slot_f, upper, 5)
            self.wait(slot_f, lower, 6)

        def across_near(self):
            self.wait(slot_yl, None, 3)
            self.send(slot_yl, upper, xr, 7, 7)
            self.wait(slot_yr, None, 4)
            self.send(slot_yr, lower, xl, 8, 8)

        def across_far(self):
            self.wait(slot_yf, upper, 7)
            self.wait(slot_yf, lower, 8)

    def wo_send(e):
        to = lax.rem(t + e, NT)
        cols = pl.ds(pl.multiple_of(to * WIDTH, WIDTH), WIDTH)
        return remote(wo_in.at[:, qtr, :, cols], wo.at[t, :, qtr], wo_ss.at[e], wo_rs.at[e], (p, to))

    def wo_start():
        for e in range(1, NT):
            go(wo_send, e)

    def wo_share(i, quarter, to):
        view = wo.at[:, :, quarter]
        return remote(view, view, wx_ss.at[i], wx_rs.at[i], to)

    def wo_pass():
        for e in range(1, NT):
            frm = lax.rem(t + NT - e, NT)
            view = wo.at[frm, :, qtr]
            remote(view, view, wo_ss.at[e], wo_rs.at[e], sibling).wait_recv()
        wo_own.wait()
        go(wo_share, 0, qtr, partner)
        go(wo_share, 1, qtr, sibling)

    other = (1 - b) * 2 + c

    def wo_pass_on():
        wo_share(0, other, partner).wait_recv()
        go(wo_share, 2, other, sibling)

    def wo_end():
        wo_share(1, b * 2 + 1 - c, sibling).wait_recv()
        wo_share(2, (1 - b) * 2 + 1 - c, sibling).wait_recv()

    def stats(slot, seen):
        xb = tok[slot].astype(F32)
        mb = jnp.sum(xb, axis=1, keepdims=True) * (1.0 / WIDTH)
        cb = xb - mb
        sb = jnp.sum(cb * cb, axis=1, keepdims=True)
        if seen == 0:
            mean_s[...] = mb
            dev_s[...] = sb
        else:
            delta = mb - mean_s[...]
            mean_s[...] += delta * (1.0 / (seen + 1))
            dev_s[...] += sb + delta * delta * (WIDTH * seen / (seen + 1))

    def finish_block(h, halves, first):
        top = halves[0][0].max(axis=0, keepdims=True)
        for s, _ in halves[1:]:
            top = jnp.maximum(top, s.max(axis=0, keepdims=True))
        if first:
            new = top
        else:
            old = m_s[h]
            new = jnp.maximum(old, top)
            alpha = jnp.exp2((old - new) * EXP_SCALE)
        m_s[h] = new
        shift_by = new * EXP_SCALE
        total, summed = None, None
        for s, times in halves:
            weights = jnp.exp2(s * EXP_SCALE - shift_by)
            part = jnp.sum(weights, axis=0, keepdims=True)
            prod = times(weights.astype(BF16))
            total = part if total is None else total + part
            summed = prod if summed is None else summed + prod
        if first:
            l_s[h] = total
            acc[h] = summed
        else:
            l_s[h] = l_s[h] * alpha + total
            acc[h] = acc[h] * alpha + summed

    def first_block(h):
        remote(
            kv.at[me, h], kv.at[me, h], d2d_ss.at[0, h], d2d_rs.at[0, h], sibling
        ).wait_recv()
        near = z * 2 + 1 - c
        query = qt[h]
        mine, theirs = query[:, :ROWS], query[:, ROWS:]
        s0 = jnp.concatenate([dot(fresh[h, 0], mine), dot(kv[me, h, 0], theirs)], axis=1)
        s1 = dot(kv[near, h, 0], query)

        def times0(weights):
            return jnp.concatenate(
                [dot_t(fresh[h, 1], weights[:, :ROWS]), dot_t(kv[me, h, 1], weights[:, ROWS:])], axis=1
            )

        finish_block(h, [(s0, times0), (s1, lambda weights: dot_t(kv[near, h, 1], weights))], True)

    def later_block(h, i):
        d = lax.div(i - 1, 2) + 1
        side = lax.rem(i - 1, 2)
        k = d + 4 * (1 - side) * (1 - lax.div(d, 4))
        chip = lax.rem(z - d * dz[0] * (1 - 2 * side) + NZ, NZ)
        slot = chip * 2 + 1 - c
        remote(
            kv.at[slot, h], kv.at[slot, h], d2d_ss.at[k, h], d2d_rs.at[k, h], sibling
        ).wait_recv()
        query = qt[h]
        halves = []
        for i in (0, 1):
            slot = chip * 2 + i
            s = dot(kv[slot, h, 0], query)
            halves.append((s, lambda weights, slot=slot: dot_t(kv[slot, h, 1], weights)))
        finish_block(h, halves, False)

    gathers = [Gather(att.at[h], att_ss.at[h], att_rs.at[h]) for h in range(NH)]

    def o_copy(h):
        return remote(osend.at[h], orecv.at[h], o_ss.at[h], o_rs.at[h], partner)

    def s_copy(h):
        return remote(ssend.at[h], srecv.at[h], st_ss.at[h], st_rs.at[h], partner)

    def q_copy(h):
        return remote(qown.at[h], qpart.at[h], q_ss.at[h], q_rs.at[h], partner)

    def give(h):
        total = l_s[h, :, ROWS:]
        osend[h] = (acc[h, :, ROWS:] / total).astype(BF16)
        ssend[h, 0:1, :] = m_s[h, :, ROWS:]
        ssend[h, 1:2, :] = total
        go(o_copy, h)
        go(s_copy, h)

    def merge(h):
        o_copy(h).wait_recv()
        s_copy(h).wait_recv()
        m1, m2 = m_s[h, :, :ROWS], srecv[h, 0:1, :]
        top = jnp.maximum(m1, m2)
        w1 = jnp.exp2((m1 - top) * EXP_SCALE)
        w2 = jnp.exp2((m2 - top) * EXP_SCALE) * srecv[h, 1:2, :]
        inv = 1.0 / (l_s[h, :, :ROWS] * w1 + w2)
        attended = acc[h, :, :ROWS] * (w1 * inv) + orecv[h].astype(F32) * (w2 * inv)
        att[h, t] = attended.T.astype(BF16)
        gathers[h].start()

    def project(h):
        total = None
        for s in range(0, NT, 2):
            lhs = jnp.concatenate([att[h, s], att[h, s + 1]], axis=1)
            rhs = jnp.concatenate(
                [wo[s, h].reshape(HD, WIDTH), wo[s + 1, h].reshape(HD, WIDTH)], axis=0
            )
            part = dot(lhs, rhs)
            total = part if total is None else total + part
        if h == 0:
            out_ref[...] = total
        else:
            out_ref[...] += total

    own_kv(0)
    loads[0].wait()
    tg = Gather(tok, tok_ss, tok_rs)
    tg.start()
    own_kv(1)
    stats(t, 0)
    event(0, 1)
    own_kv(2)
    tg.near()
    tg.across()
    stats(slot_l, 1)
    stats(slot_r, 2)
    event(0, 2)
    stats(slot_y, 3)
    event(1, 1)
    tg.far()
    stats(slot_f, 4)
    tg.across_near()
    stats(slot_yl, 5)
    stats(slot_yr, 6)
    event(0, 3)
    tg.across_far()
    wo_start()
    stats(slot_yf, 7)
    event(1, 2)
    mean = mean_s[...]
    inv = lax.rsqrt(dev_s[...] * (1.0 / D) + 1e-6)
    for i in range(NT):
        cols = slice(i * WIDTH, (i + 1) * WIDTH)
        normed = (tok[i].astype(F32) - mean) * inv
        mod[:, cols] = (normed * (1.0 + scale_ref[:, cols]) + shift_ref[:, cols]).astype(BF16)
    event(2, 1)
    for j in range(3):
        w_loads[j].wait()
        res = dot(mod[...], w[j]).astype(BF16)
        for h in range(NH):
            head = res[:, h * HD : (h + 1) * HD]
            if j == 0:
                qown[h] = head
                go(q_copy, h)
                qt[h, :, :ROWS] = head.T
            else:
                fresh[h, j - 1] = head
        if j == 0:
            event(0, 4)
        if j == 1:
            event(1, 3)
    for h in range(NH):
        q_copy(h).wait_recv()
        qt[h, :, ROWS:] = qpart[h].T

    plan = {
        2: [lambda: event(2, 2)],
        4: [lambda: event(1, 4)],
        5: [wo_pass],
        8: [lambda: give(0)],
        9: [lambda: event(2, 3)],
        11: [lambda: merge(0)],
        12: [wo_pass_on],
        13: [lambda: event(2, 4)],
        14: [lambda: gathers[0].near(), lambda: gathers[0].across()],
        16: [lambda: give(1)],
        17: [lambda: gathers[0].across_near()],
        19: [lambda: merge(1)],
        20: [lambda: gathers[0].far(), lambda: gathers[0].across_far()],
        22: [lambda: gathers[1].near(), lambda: gathers[1].across()],
    }

    def step(n, _):
        for at, todo in plan.items():

            @pl.when(n == at)
            def _(todo=todo):
                for f in todo:
                    f()

        h, i = lax.div(n, 8), lax.rem(n, 8)

        @pl.when(i == 0)
        def _():
            first_block(h)

        @pl.when(i > 0)
        def _():
            later_block(h, i)

        return 0

    lax.fori_loop(0, 8 * NH, step, 0)
    give(2)
    gathers[1].across_near()
    wo_end()
    merge(2)
    project(0)
    gathers[2].near()
    gathers[2].across()
    gathers[1].far()
    gathers[1].across_far()
    project(1)
    gathers[2].across_near()
    gathers[2].far()
    gathers[2].across_far()
    project(2)
    for make, args in sent:
        make(*args).wait_send()


def block(tokens, scale, shift, w, wo, sk, sv):
    dma, vmem = pltpu.SemaphoreType.DMA, pltpu.VMEM
    anywhere = pl.BlockSpec(memory_space=pl.ANY)
    inside = pl.BlockSpec(memory_space=pltpu.VMEM)
    return pl.pallas_call(
        kernel,
        out_shape=jax.ShapeDtypeStruct((ROWS, WIDTH), F32),
        in_specs=[anywhere, inside, inside, anywhere, anywhere, anywhere, anywhere],
        out_specs=inside,
        scratch_shapes=[
            vmem((2 * NZ, NH, 2, ROWS, HD), BF16),
            vmem((NT, ROWS, WIDTH), BF16),
            vmem((ROWS, D), BF16),
            vmem((3, D, WIDTH), BF16),
            vmem((NT, NH, 4, 32, WIDTH), BF16),
            vmem((NH, NT, ROWS, HD), BF16),
            vmem((NH, ROWS, HD), BF16),
            vmem((NH, ROWS, HD), BF16),
            vmem((NH, HD, 2 * ROWS), BF16),
            vmem((NH, 2, ROWS, HD), BF16),
            vmem((NH, 1, 2 * ROWS), F32),
            vmem((NH, 1, 2 * ROWS), F32),
            vmem((NH, HD, 2 * ROWS), F32),
            vmem((ROWS, 1), F32),
            vmem((ROWS, 1), F32),
            vmem((NH, HD, ROWS), BF16),
            vmem((NH, HD, ROWS), BF16),
            vmem((NH, 8, ROWS), F32),
            vmem((NH, 8, ROWS), F32),
            dma((8,)),
            dma((3,)),
            dma((2, NH, 4)),
            dma((2, NH, 4)),
            dma((8, NH)),
            dma((8, NH)),
            dma((9,)),
            dma((9,)),
            dma((NH, 9)),
            dma((NH, 9)),
            dma((NH,)),
            dma((NH,)),
            dma((NH,)),
            dma((NH,)),
            dma((NH,)),
            dma((NH,)),
            dma((NT,)),
            dma((NT,)),
            dma((3,)),
            dma((3,)),
        ],
        compiler_params=pltpu.CompilerParams(
            collective_id=0, has_side_effects=True, vmem_limit_bytes=56 * 1024 * 1024
        ),
        name="attention_block",
    )(tokens, scale, shift, w, wo, sk, sv)


def local(tokens, shift, scale, gate, w_qkv, w_out, stale_keys, stale_values):
    summed = block(
        tokens,
        scale.reshape(1, D),
        shift.reshape(1, D),
        jnp.transpose(w_qkv, (1, 0, 2)),
        w_out.reshape(NH, 4, 32, D),
        stale_keys,
        stale_values,
    )
    branch = gate * summed
    return ((tokens.astype(F32) + branch).astype(BF16), branch)


def solution(mesh):
    in_specs = (
        P("patch", "tensor"),
        P(),
        P(),
        P("tensor"),
        P(None, None, "tensor"),
        P("tensor", None),
        P("patch", "tensor"),
        P("patch", "tensor"),
    )
    out_specs = (P("patch", "tensor"), P("patch", "tensor"))
    return jax.shard_map(local, mesh=mesh, in_specs=in_specs, out_specs=out_specs, check_vma=False)
```

```python
import jax
import jax.numpy as jnp
from jax import lax
from jax.experimental import pallas as pl
from jax.experimental.pallas import tpu as pltpu
from jax.sharding import PartitionSpec as P

MESH = pl.DeviceIdType.MESH
HD = 128
ROWS = 256
NH = 3
WIDTH = NH * HD
D = 3072
NT = 8
NZ = 8
LOG2E = 1.4426950408889634
EXP_SCALE = LOG2E / (HD**0.5)
DEPTH = (4, 3)
FRESH = 2 * NZ
F32 = jnp.float32
BF16 = jnp.bfloat16


def dot(a, b):
    return jnp.dot(a, b, preferred_element_type=F32)


def kernel(
    tok_in, scale_ref, shift_ref, w_in, wo_in, sk_in, sv_in,
    out_ref,
    kv, vtmp, tok, mod, w, wo, wo2, att, att2, sum_out, sum_in, qown, qpart, qt, m_s, l_s, acc, sc_a, sc_b, mean_s, dev_s,
    osend, orecv, ssend, srecv,
    loc_sem, w_sem, ring_ss, ring_rs, d2d_ss, d2d_rs, tok_ss, tok_rs, att_ss, att_rs,
    q_ss, q_rs, o_ss, o_rs, st_ss, st_rs, wo_ss, wo_rs, w2_ss, w2_rs, wx_ss, wx_rs, sum_ss, sum_rs,
):
    p, t = lax.axis_index("patch"), lax.axis_index("tensor")
    b, z, c = lax.div(p, 16), lax.rem(lax.div(p, 2), NZ), lax.rem(p, 2)
    yh, x = lax.div(t, 4), lax.rem(t, 4)

    def dev(b=b, z=z, c=c, yh=yh, x=x):
        return (b * 16 + z * 2 + c, yh * 4 + x)

    def remote(src, dst, ss, rs, to):
        return pltpu.make_async_remote_copy(
            src_ref=src, dst_ref=dst, send_sem=ss, recv_sem=rs, device_id=to, device_id_type=MESH
        )

    dz = (1 - 2 * c, 2 * c - 1)
    zs = tuple(lax.rem(z + s + NZ, NZ) for s in dz)
    sibling, partner = dev(c=1 - c), dev(b=1 - b)
    xr, xl = dev(x=lax.rem(x + 1, 4)), dev(x=lax.rem(x + 3, 4))
    yo = dev(yh=1 - yh)
    me = z * 2 + c

    tok_load = pltpu.make_async_copy(tok_in, tok.at[t], loc_sem.at[0])
    k_loads, v_loads = [], []
    for h in range(NH):
        cols = pl.ds(h * HD, HD)
        k_loads.append(pltpu.make_async_copy(sk_in.at[:, cols], kv.at[me, h, 0], loc_sem.at[1 + 2 * h]))
        v_loads.append(pltpu.make_async_copy(sv_in.at[:, cols], vtmp.at[h], loc_sem.at[2 + 2 * h]))
    w_loads = [pltpu.make_async_copy(w_in.at[j], w.at[j], w_sem.at[j]) for j in range(3)]
    for copy in v_loads + k_loads + [tok_load] + w_loads:
        copy.start()

    barrier = pltpu.get_barrier_semaphore()
    peers = [sibling, partner, dev(z=zs[0]), dev(z=zs[1])]
    for e in range(1, NT):
        peers.append((p, lax.rem(t + e, NT)))
    for peer in peers:
        pl.semaphore_signal(barrier, inc=1, device_id=peer, device_id_type=MESH)

    def put_values(slot, h, values):
        kv[slot, h, 1, :HD] = values[:HD].T
        kv[slot, h, 1, HD:] = values[HD:].T

    for h in range(NH):
        v_loads[h].wait()
        put_values(me, h, vtmp[h])
    for copy in k_loads + [tok_load]:
        copy.wait()
    pl.semaphore_wait(barrier, len(peers))

    sent = []

    def go(make, *args):
        make(*args).start()
        sent.append((make, args))

    def drain():
        for make, args in sent:
            make(*args).wait_send()
        sent.clear()

    def slot_of(s, d):
        return lax.rem(z - d * dz[s] + NZ, NZ) * 2 + c

    def unit(slot, u):
        return kv.at[slot, u // 2, u % 2]

    def ring(s, u, d):
        view = unit(slot_of(s, d), u)
        return remote(view, view, ring_ss.at[s, u, d], ring_rs.at[s, u, d], dev(z=zs[s]))

    def share(k, u, slot):
        return remote(unit(slot, u), unit(slot, u), d2d_ss.at[k, u], d2d_rs.at[k, u], sibling)

    def own(u):
        go(ring, 0, u, 0)
        go(ring, 1, u, 0)
        go(share, 0, u, me)

    def event(u, d):
        for s in (0, 1):
            if d > DEPTH[s]:
                continue
            slot = slot_of(s, d)
            remote(
                unit(slot, u), unit(slot, u), ring_ss.at[s, u, d - 1], ring_rs.at[s, u, d - 1], sibling
            ).wait_recv()
            if d < DEPTH[s]:
                go(ring, s, u, d)
            go(share, d + 4 * s, u, slot)

    slot_l, slot_r, slot_f = (yh * 4 + lax.rem(x + e, 4) for e in (3, 1, 2))
    slot_y, slot_yl, slot_yr, slot_yf = ((1 - yh) * 4 + lax.rem(x + e, 4) for e in (0, 3, 1, 2))
    rows = (pl.ds(0, ROWS // 2), pl.ds(ROWS // 2, ROWS // 2))

    def tok_copy(slot, half, to, i):
        view = tok.at[slot, rows[half]]
        return remote(view, view, tok_ss.at[i], tok_rs.at[i], to)

    def tok_wait(slot, half, i):
        tok_copy(slot, half, sibling, i).wait_recv()

    def wo_cols(to):
        return pl.ds(pl.multiple_of(to * WIDTH, WIDTH), WIDTH)

    def wo_near(e, g):
        to = lax.rem(x + e, 4)
        src = wo_in.at[pl.ds(0, 2), c, :, wo_cols(g * 4 + to)]
        return remote(src, wo.at[x, g, :, c], wo_ss.at[2 * e + g], wo_rs.at[2 * e + g], dev(x=to))

    def wo_near_own(g):
        src = wo_in.at[pl.ds(0, 2), c, :, wo_cols(g * 4 + x)]
        return pltpu.make_async_copy(src, wo.at[x, g, :, c], wo_ss.at[g])

    def wo_all(e):
        to = yh * 4 + lax.rem(x + e, 4) if e < 4 else (1 - yh) * 4 + lax.rem(x + e, 4)
        src = wo_in.at[2, c, :, wo_cols(to)]
        return remote(src, wo2.at[t, c], w2_ss.at[e], w2_rs.at[e], (p, to))

    def wo_all_own():
        return pltpu.make_async_copy(wo_in.at[2, c, :, wo_cols(t)], wo2.at[t, c], w2_ss.at[0])

    def wo_share(half):
        return remote(wo.at[:, :, :, half], wo.at[:, :, :, half], wx_ss.at[0], wx_rs.at[0], sibling)

    def wo_share2(half):
        return remote(wo2.at[:, half], wo2.at[:, half], wx_ss.at[1], wx_rs.at[1], sibling)

    def wo_pass():
        for e in range(1, 4):
            for g in (0, 1):
                view = wo.at[lax.rem(x + 4 - e, 4), g, :, c]
                remote(view, view, wo_ss.at[2 * e + g], wo_rs.at[2 * e + g], sibling).wait_recv()
        for g in (0, 1):
            wo_near_own(g).wait()
        go(wo_share, c)

    def wo_pass2():
        for e in range(1, NT):
            frm = yh * 4 + lax.rem(x + 4 - e, 4) if e < 4 else (1 - yh) * 4 + lax.rem(x + 8 - e, 4)
            view = wo2.at[frm, c]
            remote(view, view, w2_ss.at[e], w2_rs.at[e], sibling).wait_recv()
        wo_all_own().wait()
        go(wo_share2, c)

    def stats(slot, seen):
        xb = tok[slot].astype(F32)
        mb = jnp.sum(xb, axis=1, keepdims=True) * (1.0 / WIDTH)
        cb = xb - mb
        sb = jnp.sum(cb * cb, axis=1, keepdims=True)
        if seen == 0:
            mean_s[...] = mb
            dev_s[...] = sb
        else:
            delta = mb - mean_s[...]
            mean_s[...] += delta * (1.0 / (seen + 1))
            dev_s[...] += sb + delta * delta * (WIDTH * seen / (seen + 1))

    def place(n):
        h, i = n // 8, n % 8
        d, side = (i + 1) // 2, (i + 1) % 2
        chip = lax.rem(z - d * dz[side] + NZ, NZ)
        if d in (0, 4):
            k = d
        else:
            k = d if side else d + 4
        return h, i, k, chip * 2 + c, chip * 2 + 1 - c

    def block_wait(n, j):
        h, _, k, _, far = place(n)
        share(k, 2 * h + j, far).wait_recv()

    def scores(n):
        h, i, _, near, far = place(n)
        buf = (sc_a, sc_b)[n % 2]
        query = qt[h]
        if i == 0:
            first = jnp.concatenate(
                [dot(kv[FRESH, h, 0], query[:, :ROWS]), dot(kv[near, h, 0], query[:, ROWS:])], axis=1
            )
        else:
            first = dot(kv[near, h, 0], query)
        top = None
        for j, s in enumerate((first, dot(kv[far, h, 0], query))):
            s = s * EXP_SCALE
            buf[j] = s
            part = s.max(axis=0, keepdims=True)
            top = part if top is None else jnp.maximum(top, part)
        return top

    def values(slot, h):
        return jnp.concatenate([kv[slot, h, 1, :HD], kv[slot, h, 1, HD:]], axis=1)

    def weigh(n, top):
        h, i, _, near, far = place(n)
        buf = (sc_a, sc_b)[n % 2]
        new = top if i == 0 else jnp.maximum(m_s[h], top)
        total, summed = None, None
        for j, slot in enumerate((near, far)):
            weights = jnp.exp2(buf[j] - new)
            part = jnp.sum(weights, axis=0, keepdims=True)
            weights = weights.astype(BF16)
            if i == 0 and j == 0:
                prod = jnp.concatenate(
                    [dot(values(FRESH, h), weights[:, :ROWS]), dot(values(slot, h), weights[:, ROWS:])], axis=1
                )
            else:
                prod = dot(values(slot, h), weights)
            total = part if total is None else total + part
            summed = prod if summed is None else summed + prod
        if i == 0:
            l_s[h] = total
            acc[h] = summed
        else:
            alpha = jnp.exp2(m_s[h] - new)
            l_s[h] = l_s[h] * alpha + total
            acc[h] = acc[h] * alpha + summed
        m_s[h] = new

    def o_copy(h):
        return remote(osend.at[h], orecv.at[h], o_ss.at[h], o_rs.at[h], partner)

    def s_copy(h):
        return remote(ssend.at[h], srecv.at[h], st_ss.at[h], st_rs.at[h], partner)

    def q_copy(h):
        return remote(qown.at[h], qpart.at[h], q_ss.at[h], q_rs.at[h], partner)

    def give(h):
        total = l_s[h, :, ROWS:]
        osend[h] = (acc[h, :, ROWS:] / total).astype(BF16)
        ssend[h, 0:1, :] = m_s[h, :, ROWS:]
        ssend[h, 1:2, :] = total
        go(o_copy, h)
        go(s_copy, h)

    def att_copy(h, e):
        if h < 2:
            view, to = att.at[h, x], dev(x=lax.rem(x + e, 4))
        else:
            view, to = att2.at[t], (p, lax.rem(t + e, NT))
        return remote(view, view, att_ss.at[h, e], att_rs.at[h, e], to)

    def att_wait(h):
        for e in range(1, 4 if h < 2 else NT):
            view = att.at[h, lax.rem(x + 4 - e, 4)] if h < 2 else att2.at[lax.rem(t + NT - e, NT)]
            remote(view, view, att_ss.at[h, e], att_rs.at[h, e], sibling).wait_recv()

    def merge(h):
        o_copy(h).wait_recv()
        s_copy(h).wait_recv()
        m1, m2 = m_s[h, :, :ROWS], srecv[h, 0:1, :]
        top = jnp.maximum(m1, m2)
        w1 = jnp.exp2(m1 - top)
        w2 = jnp.exp2(m2 - top) * srecv[h, 1:2, :]
        inv = 1.0 / (l_s[h, :, :ROWS] * w1 + w2)
        attended = acc[h, :, :ROWS] * (w1 * inv) + orecv[h].astype(F32) * (w2 * inv)
        attended = attended.T.astype(BF16)
        if h < 2:
            att[h, x] = attended
        else:
            att2[t] = attended
        for e in range(1, 4 if h < 2 else NT):
            go(att_copy, h, e)

    def project(g):
        total = None
        for s in range(4):
            lhs = jnp.concatenate([att[0, s], att[1, s]], axis=1)
            part = dot(lhs, wo[s, g].reshape(2 * HD, WIDTH))
            total = part if total is None else total + part
        return total

    def project_last():
        total = None
        for s in range(0, NT, 2):
            lhs = jnp.concatenate([att2[s], att2[s + 1]], axis=1)
            part = dot(lhs, wo2[pl.ds(s, 2)].reshape(2 * HD, WIDTH))
            total = part if total is None else total + part
        return total

    def sum_copy():
        return remote(sum_out, sum_in, sum_ss.at[0], sum_rs.at[0], yo)

    for u in range(5):
        own(u)
    for i in (0, 1):
        go(tok_copy, t, i, yo, 4 + i)
        go(tok_copy, t, i, xr, 0 + i)
        go(tok_copy, t, i, xl, 2 + i)
    stats(t, 0)
    tok_wait(slot_l, 0, 0)
    go(tok_copy, slot_l, 0, xr, 6)
    tok_wait(slot_y, 0, 4)
    go(tok_copy, slot_y, 0, xr, 8)
    go(tok_copy, slot_y, 0, xl, 10)
    tok_wait(slot_r, 1, 3)
    go(tok_copy, slot_r, 1, xl, 7)
    tok_wait(slot_y, 1, 5)
    go(tok_copy, slot_y, 1, xr, 9)
    go(tok_copy, slot_y, 1, xl, 11)
    event(0, 1)
    event(1, 1)
    event(2, 1)
    own(5)
    tok_wait(slot_l, 1, 1)
    tok_wait(slot_r, 0, 2)
    stats(slot_l, 1)
    stats(slot_r, 2)
    tok_wait(slot_f, 0, 6)
    go(tok_copy, slot_f, 0, yo, 12)
    tok_wait(slot_f, 1, 7)
    go(tok_copy, slot_f, 1, yo, 13)
    stats(slot_y, 3)
    stats(slot_f, 4)
    event(0, 2)
    event(1, 2)
    event(3, 1)
    for i in (0, 1):
        tok_wait(slot_yl, i, 8 + i)
        tok_wait(slot_yr, i, 10 + i)
    stats(slot_yl, 5)
    stats(slot_yr, 6)
    event(2, 2)
    tok_wait(slot_yf, 0, 12)
    tok_wait(slot_yf, 1, 13)
    stats(slot_yf, 7)
    for g in (0, 1):
        wo_near_own(g).start()
        for e in (1, 2, 3):
            go(wo_near, e, g)
    wo_all_own().start()
    for e in (1, 2, 3):
        go(wo_all, e)
    mean = mean_s[...]
    inv = lax.rsqrt(dev_s[...] * (1.0 / D) + 1e-6)
    for i in range(NT):
        cols = slice(i * WIDTH, (i + 1) * WIDTH)
        normed = (tok[i].astype(F32) - mean) * inv
        mod[:, cols] = (normed * (1.0 + scale_ref[:, cols]) + shift_ref[:, cols]).astype(BF16)
    after = {0: [(0, 3), (1, 3)], 1: [(4, 1), (3, 2)], 2: [(5, 1), (2, 3)]}
    for j in range(3):
        w_loads[j].wait()
        res = dot(mod[...], w[j]).astype(BF16)
        for h in range(NH):
            head = res[:, h * HD : (h + 1) * HD]
            if j == 0:
                qown[h] = head
                go(q_copy, h)
                qt[h, :, :ROWS] = head.T
            elif j == 1:
                kv[FRESH, h, 0] = head
            else:
                put_values(FRESH, h, head)
        for u, d in after[j]:
            event(u, d)
    for h in range(NH):
        q_copy(h).wait_recv()
        qt[h, :, ROWS:] = qpart[h].T
    for e in (4, 5, 6, 7):
        go(wo_all, e)

    before = {
        1: [(0, 4), (1, 4)],
        3: [(4, 2), (3, 3)],
        6: [(5, 2), (2, 4)],
        9: [(4, 3)],
        11: [(3, 4)],
        13: [(5, 3)],
        20: [(4, 4)],
        21: [(5, 4)],
    }
    extra = {
        8: lambda: give(0),
        15: lambda: merge(0),
        16: lambda: give(1),
        18: wo_pass,
        19: wo_pass2,
        21: lambda: merge(1),
    }
    block_wait(0, 0)
    top = scores(0)
    for n in range(8 * NH):
        for u, d in before.get(n, ()):
            event(u, d)
        if n in extra:
            extra[n]()
        block_wait(n, 1)
        if n + 1 < 8 * NH:
            block_wait(n + 1, 0)
            later = scores(n + 1)
        weigh(n, top)
        top = later
    give(2)
    att_wait(0)
    att_wait(1)
    wo_share(1 - c).wait_recv()
    sum_out[...] = project(1 - yh).astype(BF16)
    go(sum_copy)
    out_ref[...] = project(yh)
    merge(2)
    wo_share2(1 - c).wait_recv()
    sum_copy().wait_recv()
    out_ref[...] += sum_in[...].astype(F32)
    drain()
    att_wait(2)
    out_ref[...] += project_last()


def block(tokens, scale, shift, w, wo, sk, sv):
    dma, vmem = pltpu.SemaphoreType.DMA, pltpu.VMEM
    anywhere = pl.BlockSpec(memory_space=pl.ANY)
    inside = pl.BlockSpec(memory_space=pltpu.VMEM)
    return pl.pallas_call(
        kernel,
        out_shape=jax.ShapeDtypeStruct((ROWS, WIDTH), F32),
        in_specs=[anywhere, inside, inside, anywhere, anywhere, anywhere, anywhere],
        out_specs=inside,
        scratch_shapes=[
            vmem((2 * NZ + 1, NH, 2, ROWS, HD), BF16),
            vmem((NH, ROWS, HD), BF16),
            vmem((NT, ROWS, WIDTH), BF16),
            vmem((ROWS, D), BF16),
            vmem((3, D, WIDTH), BF16),
            vmem((4, 2, 2, 2, 64, WIDTH), BF16),
            vmem((NT, 2, 64, WIDTH), BF16),
            vmem((2, 4, ROWS, HD), BF16),
            vmem((NT, ROWS, HD), BF16),
            vmem((ROWS, WIDTH), BF16),
            vmem((ROWS, WIDTH), BF16),
            vmem((NH, ROWS, HD), BF16),
            vmem((NH, ROWS, HD), BF16),
            vmem((NH, HD, 2 * ROWS), BF16),
            vmem((NH, 1, 2 * ROWS), F32),
            vmem((NH, 1, 2 * ROWS), F32),
            vmem((NH, HD, 2 * ROWS), F32),
            vmem((2, ROWS, 2 * ROWS), F32),
            vmem((2, ROWS, 2 * ROWS), F32),
            vmem((ROWS, 1), F32),
            vmem((ROWS, 1), F32),
            vmem((NH, HD, ROWS), BF16),
            vmem((NH, HD, ROWS), BF16),
            vmem((NH, 8, ROWS), F32),
            vmem((NH, 8, ROWS), F32),
            dma((8,)),
            dma((3,)),
            dma((2, 2 * NH, 4)),
            dma((2, 2 * NH, 4)),
            dma((8, 2 * NH)),
            dma((8, 2 * NH)),
            dma((14,)),
            dma((14,)),
            dma((NH, NT)),
            dma((NH, NT)),
            dma((NH,)),
            dma((NH,)),
            dma((NH,)),
            dma((NH,)),
            dma((NH,)),
            dma((NH,)),
            dma((NT,)),
            dma((NT,)),
            dma((NT,)),
            dma((NT,)),
            dma((2,)),
            dma((2,)),
            dma((1,)),
            dma((1,)),
        ],
        compiler_params=pltpu.CompilerParams(
            collective_id=0, has_side_effects=True, vmem_limit_bytes=56 * 1024 * 1024
        ),
        name="attention_block",
    )(tokens, scale, shift, w, wo, sk, sv)


def local(tokens, shift, scale, gate, w_qkv, w_out, stale_keys, stale_values):
    summed = block(
        tokens,
        scale.reshape(1, D),
        shift.reshape(1, D),
        jnp.transpose(w_qkv, (1, 0, 2)),
        w_out.reshape(NH, 2, 64, D),
        stale_keys,
        stale_values,
    )
    branch = gate * summed
    return ((tokens.astype(F32) + branch).astype(BF16), branch)


def solution(mesh):
    in_specs = (
        P("patch", "tensor"),
        P(),
        P(),
        P("tensor"),
        P(None, None, "tensor"),
        P("tensor", None),
        P("patch", "tensor"),
        P("patch", "tensor"),
    )
    out_specs = (P("patch", "tensor"), P("patch", "tensor"))
    return jax.shard_map(local, mesh=mesh, in_specs=in_specs, out_specs=out_specs, check_vma=False)
```

```python
import jax
import jax.numpy as jnp
from jax import lax
from jax.experimental import pallas as pl
from jax.experimental.pallas import tpu as pltpu
from jax.sharding import PartitionSpec as P

MESH = pl.DeviceIdType.MESH
HD = 128
ROWS = 256
NH = 3
WIDTH = NH * HD
D = 3072
NT = 8
NZ = 8
LOG2E = 1.4426950408889634
EXP_SCALE = LOG2E / (HD**0.5)
DEPTH = (4, 3)
FRESH = 2 * NZ
F32 = jnp.float32
BF16 = jnp.bfloat16


def dot(a, b):
    return jnp.dot(a, b, preferred_element_type=F32)


def kernel(
    tok_in, scale_in, shift_in, w_in, wo_in, sk_in, sv_in,
    out_ref,
    scale_ref, shift_ref, kv, vtmp, tok, mod, w, wo, wo2, att, att2, sum_out, sum_in, qown, qpart, qt, m_s, l_s, acc, sc_a, sc_b, mean_s, dev_s,
    osend, orecv, ssend, srecv,
    loc_sem, w_sem, ring_ss, ring_rs, d2d_ss, d2d_rs, tok_ss, tok_rs, att_ss, att_rs,
    q_ss, q_rs, o_ss, o_rs, st_ss, st_rs, wo_ss, wo_rs, w2_ss, w2_rs, wx_ss, wx_rs, sum_ss, sum_rs,
):
    p, t = lax.axis_index("patch"), lax.axis_index("tensor")
    b, z, c = lax.div(p, 16), lax.rem(lax.div(p, 2), NZ), lax.rem(p, 2)
    yh, x = lax.div(t, 4), lax.rem(t, 4)

    def dev(b=b, z=z, c=c, yh=yh, x=x):
        return (b * 16 + z * 2 + c, yh * 4 + x)

    def remote(src, dst, ss, rs, to):
        return pltpu.make_async_remote_copy(
            src_ref=src, dst_ref=dst, send_sem=ss, recv_sem=rs, device_id=to, device_id_type=MESH
        )

    dz = (1 - 2 * c, 2 * c - 1)
    zs = tuple(lax.rem(z + s + NZ, NZ) for s in dz)
    sibling, partner = dev(c=1 - c), dev(b=1 - b)
    xr, xl = dev(x=lax.rem(x + 1, 4)), dev(x=lax.rem(x + 3, 4))
    yo = dev(yh=1 - yh)
    me = z * 2 + c

    barrier = pltpu.get_barrier_semaphore()
    peers = [sibling, partner, dev(z=zs[0]), dev(z=zs[1])]
    for e in range(1, NT):
        peers.append((p, lax.rem(t + e, NT)))
    for peer in peers:
        pl.semaphore_signal(barrier, inc=1, device_id=peer, device_id_type=MESH)

    tok_load = pltpu.make_async_copy(tok_in, tok.at[t], loc_sem.at[0])
    k_loads, v_loads = [], []
    for h in range(NH):
        cols = pl.ds(h * HD, HD)
        k_loads.append(pltpu.make_async_copy(sk_in.at[:, cols], kv.at[me, h, 0], loc_sem.at[1 + 2 * h]))
        v_loads.append(pltpu.make_async_copy(sv_in.at[:, cols], vtmp.at[h], loc_sem.at[2 + 2 * h]))
    vec_loads = [
        pltpu.make_async_copy(scale_in, scale_ref, loc_sem.at[7]),
        pltpu.make_async_copy(shift_in, shift_ref, loc_sem.at[8]),
    ]
    w_loads = [pltpu.make_async_copy(w_in.at[j], w.at[j], w_sem.at[j]) for j in range(3)]
    for copy in v_loads + k_loads + [tok_load] + vec_loads + w_loads:
        copy.start()

    def put_values(slot, h, values):
        kv[slot, h, 1, :HD] = values[:HD].T
        kv[slot, h, 1, HD:] = values[HD:].T

    for h in range(NH):
        v_loads[h].wait()
        put_values(me, h, vtmp[h])
    for copy in k_loads + [tok_load]:
        copy.wait()
    pl.semaphore_wait(barrier, len(peers))

    sent = []

    def go(make, *args):
        make(*args).start()
        sent.append((make, args))

    def drain():
        for make, args in sent:
            make(*args).wait_send()
        sent.clear()

    def slot_of(s, d):
        return lax.rem(z - d * dz[s] + NZ, NZ) * 2 + c

    def unit(slot, u):
        return kv.at[slot, u // 2, u % 2]

    def ring(s, u, d):
        view = unit(slot_of(s, d), u)
        return remote(view, view, ring_ss.at[s, u, d], ring_rs.at[s, u, d], dev(z=zs[s]))

    def share(k, u, slot):
        return remote(unit(slot, u), unit(slot, u), d2d_ss.at[k, u], d2d_rs.at[k, u], sibling)

    def own(u):
        go(ring, 0, u, 0)
        go(ring, 1, u, 0)
        go(share, 0, u, me)

    def event(u, d):
        for s in (0, 1):
            if d > DEPTH[s]:
                continue
            slot = slot_of(s, d)
            remote(
                unit(slot, u), unit(slot, u), ring_ss.at[s, u, d - 1], ring_rs.at[s, u, d - 1], sibling
            ).wait_recv()
            if d < DEPTH[s]:
                go(ring, s, u, d)
            go(share, d + 4 * s, u, slot)

    slot_l, slot_r, slot_f = (yh * 4 + lax.rem(x + e, 4) for e in (3, 1, 2))
    slot_y, slot_yl, slot_yr, slot_yf = ((1 - yh) * 4 + lax.rem(x + e, 4) for e in (0, 3, 1, 2))
    rows = (pl.ds(0, ROWS // 2), pl.ds(ROWS // 2, ROWS // 2))

    def tok_copy(slot, half, to, i):
        view = tok.at[slot, rows[half]]
        return remote(view, view, tok_ss.at[i], tok_rs.at[i], to)

    def tok_wait(slot, half, i):
        tok_copy(slot, half, sibling, i).wait_recv()

    def wo_cols(to):
        return pl.ds(pl.multiple_of(to * WIDTH, WIDTH), WIDTH)

    def wo_near(e, g):
        to = lax.rem(x + e, 4)
        src = wo_in.at[pl.ds(0, 2), c, :, wo_cols(g * 4 + to)]
        return remote(src, wo.at[x, g, :, c], wo_ss.at[2 * e + g], wo_rs.at[2 * e + g], dev(x=to))

    def wo_near_own(g):
        src = wo_in.at[pl.ds(0, 2), c, :, wo_cols(g * 4 + x)]
        return pltpu.make_async_copy(src, wo.at[x, g, :, c], wo_ss.at[g])

    def wo_all(e):
        to = yh * 4 + lax.rem(x + e, 4) if e < 4 else (1 - yh) * 4 + lax.rem(x + e, 4)
        src = wo_in.at[2, c, :, wo_cols(to)]
        return remote(src, wo2.at[t, c], w2_ss.at[e], w2_rs.at[e], (p, to))

    def wo_all_own():
        return pltpu.make_async_copy(wo_in.at[2, c, :, wo_cols(t)], wo2.at[t, c], w2_ss.at[0])

    def wo_share(half):
        return remote(wo.at[:, :, :, half], wo.at[:, :, :, half], wx_ss.at[0], wx_rs.at[0], sibling)

    def wo_share2(half):
        return remote(wo2.at[:, half], wo2.at[:, half], wx_ss.at[1], wx_rs.at[1], sibling)

    def wo_pass():
        for e in range(1, 4):
            for g in (0, 1):
                view = wo.at[lax.rem(x + 4 - e, 4), g, :, c]
                remote(view, view, wo_ss.at[2 * e + g], wo_rs.at[2 * e + g], sibling).wait_recv()
        for g in (0, 1):
            wo_near_own(g).wait()
        go(wo_share, c)

    def wo_pass2():
        for e in range(1, NT):
            frm = yh * 4 + lax.rem(x + 4 - e, 4) if e < 4 else (1 - yh) * 4 + lax.rem(x + 8 - e, 4)
            view = wo2.at[frm, c]
            remote(view, view, w2_ss.at[e], w2_rs.at[e], sibling).wait_recv()
        wo_all_own().wait()
        go(wo_share2, c)

    def stats(slot, seen):
        xb = tok[slot].astype(F32)
        mb = jnp.sum(xb, axis=1, keepdims=True) * (1.0 / WIDTH)
        cb = xb - mb
        sb = jnp.sum(cb * cb, axis=1, keepdims=True)
        if seen == 0:
            mean_s[...] = mb
            dev_s[...] = sb
        else:
            delta = mb - mean_s[...]
            mean_s[...] += delta * (1.0 / (seen + 1))
            dev_s[...] += sb + delta * delta * (WIDTH * seen / (seen + 1))

    def place(h, i):
        d, side = (i + 1) // 2, (i + 1) % 2
        chip = lax.rem(z - d * dz[side] + NZ, NZ)
        if d in (0, 4):
            k = d
        else:
            k = d if side else d + 4
        return k, chip * 2 + c, chip * 2 + 1 - c

    def block_wait(h, i, j):
        k, _, far = place(h, i)
        share(k, 2 * h + j, far).wait_recv()

    def scores(h, i, lo, hi, buf):
        _, near, far = place(h, i)
        query = qt[h, :, lo:hi]
        if i == 0:
            parts = []
            if lo == 0:
                parts.append(dot(kv[FRESH, h, 0], query[:, :ROWS]))
            if hi > ROWS:
                parts.append(dot(kv[near, h, 0], query[:, ROWS - lo :]))
            first = parts[0] if len(parts) == 1 else jnp.concatenate(parts, axis=1)
        else:
            first = dot(kv[near, h, 0], query)
        top = None
        for j, s in enumerate((first, dot(kv[far, h, 0], query))):
            s = s * EXP_SCALE
            buf[j, :, lo:hi] = s
            part = s.max(axis=0, keepdims=True)
            top = part if top is None else jnp.maximum(top, part)
        return top

    def values(slot, h):
        return jnp.concatenate([kv[slot, h, 1, :HD], kv[slot, h, 1, HD:]], axis=1)

    def weigh(h, i, lo, hi, buf, top):
        _, near, far = place(h, i)
        new = top if i == 0 else jnp.maximum(m_s[h, :, lo:hi], top)
        total, summed = None, None
        for j, slot in enumerate((near, far)):
            weights = jnp.exp2(buf[j, :, lo:hi] - new)
            part = jnp.sum(weights, axis=0, keepdims=True)
            weights = weights.astype(BF16)
            if i == 0 and j == 0:
                parts = []
                if lo == 0:
                    parts.append(dot(values(FRESH, h), weights[:, :ROWS]))
                if hi > ROWS:
                    parts.append(dot(values(slot, h), weights[:, ROWS - lo :]))
                prod = parts[0] if len(parts) == 1 else jnp.concatenate(parts, axis=1)
            else:
                prod = dot(values(slot, h), weights)
            total = part if total is None else total + part
            summed = prod if summed is None else summed + prod
        if i == 0:
            l_s[h, :, lo:hi] = total
            acc[h, :, lo:hi] = summed
        else:
            alpha = jnp.exp2(m_s[h, :, lo:hi] - new)
            l_s[h, :, lo:hi] = l_s[h, :, lo:hi] * alpha + total
            acc[h, :, lo:hi] = acc[h, :, lo:hi] * alpha + summed
        m_s[h, :, lo:hi] = new

    def o_copy(h):
        return remote(osend.at[h], orecv.at[h], o_ss.at[h], o_rs.at[h], partner)

    def s_copy(h):
        return remote(ssend.at[h], srecv.at[h], st_ss.at[h], st_rs.at[h], partner)

    def q_copy(h):
        return remote(qown.at[h], qpart.at[h], q_ss.at[h], q_rs.at[h], partner)

    def give(h):
        total = l_s[h, :, ROWS:]
        osend[h] = (acc[h, :, ROWS:] / total).astype(BF16)
        ssend[h, 0:1, :] = m_s[h, :, ROWS:]
        ssend[h, 1:2, :] = total
        go(o_copy, h)
        go(s_copy, h)

    def att_copy(h, e):
        if h < 2:
            view, to = att.at[h, x], dev(x=lax.rem(x + e, 4))
        else:
            view = att2.at[t]
            to = yo if e == 4 else dev(x=lax.rem(x + e, 4))
        return remote(view, view, att_ss.at[h, e], att_rs.at[h, e], to)

    def att_pass(e):
        view = att2.at[slot_y]
        return remote(view, view, att_ss.at[2, 4 + e], att_rs.at[2, 4 + e], dev(x=lax.rem(x + e, 4)))

    def att_wait(h, e):
        if h < 2:
            view = att.at[h, lax.rem(x + 4 - e, 4)]
        elif e < 4:
            view = att2.at[yh * 4 + lax.rem(x + 4 - e, 4)]
        else:
            view = att2.at[(1 - yh) * 4 + lax.rem(x + 8 - e, 4)]
        remote(view, view, att_ss.at[h, e], att_rs.at[h, e], sibling).wait_recv()

    def merge(h):
        o_copy(h).wait_recv()
        s_copy(h).wait_recv()
        m1, m2 = m_s[h, :, :ROWS], srecv[h, 0:1, :]
        top = jnp.maximum(m1, m2)
        w1 = jnp.exp2(m1 - top)
        w2 = jnp.exp2(m2 - top) * srecv[h, 1:2, :]
        inv = 1.0 / (l_s[h, :, :ROWS] * w1 + w2)
        attended = acc[h, :, :ROWS] * (w1 * inv) + orecv[h].astype(F32) * (w2 * inv)
        attended = attended.T.astype(BF16)
        if h < 2:
            att[h, x] = attended
        else:
            att2[t] = attended
        for e in (1, 3, 2) if h < 2 else (4, 1, 3, 2):
            go(att_copy, h, e)

    def project(g):
        total = None
        for s in range(4):
            lhs = jnp.concatenate([att[0, s], att[1, s]], axis=1)
            part = dot(lhs, wo[s, g].reshape(2 * HD, WIDTH))
            total = part if total is None else total + part
        return total

    def project_last():
        total = None
        for s in range(0, NT, 2):
            lhs = jnp.concatenate([att2[s], att2[s + 1]], axis=1)
            part = dot(lhs, wo2[pl.ds(s, 2)].reshape(2 * HD, WIDTH))
            total = part if total is None else total + part
        return total

    def sum_copy():
        return remote(sum_out, sum_in, sum_ss.at[0], sum_rs.at[0], yo)

    for i in (0, 1):
        go(tok_copy, t, i, yo, 4 + i)
        go(tok_copy, t, i, xr, 0 + i)
        go(tok_copy, t, i, xl, 2 + i)
    for u in range(4):
        own(u)
    stats(t, 0)
    tok_wait(slot_l, 0, 0)
    go(tok_copy, slot_l, 0, xr, 6)
    tok_wait(slot_y, 0, 4)
    go(tok_copy, slot_y, 0, xr, 8)
    go(tok_copy, slot_y, 0, xl, 10)
    event(0, 1)
    tok_wait(slot_r, 1, 3)
    go(tok_copy, slot_r, 1, xl, 7)
    tok_wait(slot_y, 1, 5)
    go(tok_copy, slot_y, 1, xr, 9)
    go(tok_copy, slot_y, 1, xl, 11)
    event(1, 1)
    event(2, 1)
    tok_wait(slot_l, 1, 1)
    tok_wait(slot_r, 0, 2)
    tok_wait(slot_f, 0, 6)
    go(tok_copy, slot_f, 0, yo, 12)
    tok_wait(slot_f, 1, 7)
    go(tok_copy, slot_f, 1, yo, 13)
    event(3, 1)
    own(4)
    own(5)
    stats(slot_l, 1)
    stats(slot_r, 2)
    stats(slot_y, 3)
    stats(slot_f, 4)
    event(0, 2)
    event(1, 2)
    for i in (0, 1):
        tok_wait(slot_yl, i, 8 + i)
        tok_wait(slot_yr, i, 10 + i)
    stats(slot_yl, 5)
    stats(slot_yr, 6)
    event(2, 2)
    tok_wait(slot_yf, 0, 12)
    tok_wait(slot_yf, 1, 13)
    stats(slot_yf, 7)
    for g in (0, 1):
        wo_near_own(g).start()
        for e in (1, 2, 3):
            go(wo_near, e, g)
    wo_all_own().start()
    for e in (1, 2, 3):
        go(wo_all, e)
    for copy in vec_loads:
        copy.wait()
    mean = mean_s[...]
    inv = lax.rsqrt(dev_s[...] * (1.0 / D) + 1e-6)
    after = {0: [(3, 2)], 1: [(4, 1)], 2: [(5, 1)]}
    for j in range(3):
        w_loads[j].wait()
        if j == 0:
            res = None
            for i in range(NT):
                cols = slice(i * WIDTH, (i + 1) * WIDTH)
                normed = (tok[i].astype(F32) - mean) * inv
                slab = (normed * (1.0 + scale_ref[:, cols]) + shift_ref[:, cols]).astype(BF16)
                mod[:, cols] = slab
                part = dot(slab, w[0, cols])
                res = part if res is None else res + part
        else:
            res = dot(mod[...], w[j])
        res = res.astype(BF16)
        for h in range(NH):
            head = res[:, h * HD : (h + 1) * HD]
            if j == 0:
                qown[h] = head
                go(q_copy, h)
                qt[h, :, :ROWS] = head.T
            elif j == 1:
                kv[FRESH, h, 0] = head
            else:
                put_values(FRESH, h, head)
        for u, d in after[j]:
            event(u, d)
    for e in (4, 5, 6, 7):
        go(wo_all, e)

    def query_in(h):
        q_copy(h).wait_recv()
        qt[h, :, ROWS:] = qpart[h].T

    order = [(0, i, 0, ROWS) for i in range(5)] + [(0, i, ROWS, 2 * ROWS) for i in range(5)]
    rest = [(1, i) for i in range(5)] + [(2, 0), (2, 1), (2, 2)]
    rest += [(0, 5), (0, 6), (1, 5), (1, 6), (0, 7), (1, 7)] + [(2, i) for i in range(3, 8)]
    order += [(h, i, 0, 2 * ROWS) for h, i in rest]
    due = {
        (0, 0, 0): [lambda: event(0, 3)],
        (0, 0, ROWS): [lambda: query_in(0), lambda: event(1, 3)],
        (1, 0, 0): [lambda: query_in(1)],
        (1, 1, 0): [lambda: event(2, 3)],
        (1, 3, 0): [lambda: event(3, 3)],
        (1, 4, 0): [lambda: event(4, 2)],
        (2, 0, 0): [lambda: query_in(2)],
        (2, 2, 0): [lambda: event(5, 2)],
        (0, 6, 0): [lambda: event(0, 4)],
        (1, 5, 0): [lambda: event(1, 4)],
        (1, 6, 0): [lambda: event(2, 4)],
        (0, 7, 0): [lambda: event(3, 4), lambda: event(4, 3)],
        (2, 3, 0): [lambda: give(0), lambda: event(5, 3)],
        (2, 4, 0): [lambda: give(1), wo_pass],
        (2, 5, 0): [wo_pass2],
        (2, 6, 0): [lambda: event(4, 4), lambda: merge(0)],
        (2, 7, 0): [lambda: merge(1), lambda: event(5, 4)],
    }
    groups = [0, 5, 10, 12, 14, 16, 18, 20] + list(range(21, len(order) + 1))
    bufs = (sc_a, sc_b)
    waited = set()

    def ready(n, j):
        h, i, lo, _ = order[n]
        if j == 0:
            for f in due.get((h, i, lo), ()):
                f()
        if (h, i, j) not in waited:
            waited.add((h, i, j))
            block_wait(h, i, j)

    fresh_start = (0, 5)
    for start, stop in zip(groups, groups[1:]):
        last = stop if stop in fresh_start or stop == len(order) else stop + 1
        for n in range(start if start in fresh_start else start + 1, last):
            ready(n, 0)
        for n in range(start, stop):
            ready(n, 1)
        if start in fresh_start:
            top = scores(*order[start], bufs[start % 2])
        for n in range(start, stop):
            if n + 1 < last:
                later = scores(*order[n + 1], bufs[(n + 1) % 2])
            weigh(*order[n], bufs[n % 2], top)
            top = later
    give(2)
    wo_share(1 - c).wait_recv()
    merge(2)
    for h in (0, 1):
        for e in (1, 2, 3):
            att_wait(h, e)
    sum_out[...] = project(1 - yh).astype(BF16)
    go(sum_copy)
    out_ref[...] = project(yh)
    att_wait(2, 4)
    for e in (1, 3, 2):
        go(att_pass, e)
    for e in (1, 2, 3):
        att_wait(2, e)
    wo_share2(1 - c).wait_recv()
    sum_copy().wait_recv()
    out_ref[...] += sum_in[...].astype(F32)
    drain()
    for e in (5, 6, 7):
        att_wait(2, e)
    out_ref[...] += project_last()


def block(tokens, scale, shift, w, wo, sk, sv):
    dma, vmem = pltpu.SemaphoreType.DMA, pltpu.VMEM
    anywhere = pl.BlockSpec(memory_space=pl.ANY)
    inside = pl.BlockSpec(memory_space=pltpu.VMEM)
    return pl.pallas_call(
        kernel,
        out_shape=jax.ShapeDtypeStruct((ROWS, WIDTH), F32),
        in_specs=[anywhere] * 7,
        out_specs=inside,
        scratch_shapes=[
            vmem((1, D), F32),
            vmem((1, D), F32),
            vmem((2 * NZ + 1, NH, 2, ROWS, HD), BF16),
            vmem((NH, ROWS, HD), BF16),
            vmem((NT, ROWS, WIDTH), BF16),
            vmem((ROWS, D), BF16),
            vmem((3, D, WIDTH), BF16),
            vmem((4, 2, 2, 2, 64, WIDTH), BF16),
            vmem((NT, 2, 64, WIDTH), BF16),
            vmem((2, 4, ROWS, HD), BF16),
            vmem((NT, ROWS, HD), BF16),
            vmem((ROWS, WIDTH), BF16),
            vmem((ROWS, WIDTH), BF16),
            vmem((NH, ROWS, HD), BF16),
            vmem((NH, ROWS, HD), BF16),
            vmem((NH, HD, 2 * ROWS), BF16),
            vmem((NH, 1, 2 * ROWS), F32),
            vmem((NH, 1, 2 * ROWS), F32),
            vmem((NH, HD, 2 * ROWS), F32),
            vmem((2, ROWS, 2 * ROWS), F32),
            vmem((2, ROWS, 2 * ROWS), F32),
            vmem((ROWS, 1), F32),
            vmem((ROWS, 1), F32),
            vmem((NH, HD, ROWS), BF16),
            vmem((NH, HD, ROWS), BF16),
            vmem((NH, 8, ROWS), F32),
            vmem((NH, 8, ROWS), F32),
            dma((9,)),
            dma((3,)),
            dma((2, 2 * NH, 4)),
            dma((2, 2 * NH, 4)),
            dma((8, 2 * NH)),
            dma((8, 2 * NH)),
            dma((14,)),
            dma((14,)),
            dma((NH, NT)),
            dma((NH, NT)),
            dma((NH,)),
            dma((NH,)),
            dma((NH,)),
            dma((NH,)),
            dma((NH,)),
            dma((NH,)),
            dma((NT,)),
            dma((NT,)),
            dma((NT,)),
            dma((NT,)),
            dma((2,)),
            dma((2,)),
            dma((1,)),
            dma((1,)),
        ],
        compiler_params=pltpu.CompilerParams(
            collective_id=0, has_side_effects=True, vmem_limit_bytes=56 * 1024 * 1024
        ),
        name="attention_block",
    )(tokens, scale, shift, w, wo, sk, sv)


def local(tokens, shift, scale, gate, w_qkv, w_out, stale_keys, stale_values):
    summed = block(
        tokens,
        scale.reshape(1, D),
        shift.reshape(1, D),
        jnp.transpose(w_qkv, (1, 0, 2)),
        w_out.reshape(NH, 2, 64, D),
        stale_keys,
        stale_values,
    )
    branch = gate * summed
    return ((tokens.astype(F32) + branch).astype(BF16), branch)


def solution(mesh):
    in_specs = (
        P("patch", "tensor"),
        P(),
        P(),
        P("tensor"),
        P(None, None, "tensor"),
        P("tensor", None),
        P("patch", "tensor"),
        P("patch", "tensor"),
    )
    out_specs = (P("patch", "tensor"), P("patch", "tensor"))
    return jax.shard_map(local, mesh=mesh, in_specs=in_specs, out_specs=out_specs, check_vma=False)
```

```python
import jax
import jax.numpy as jnp
from jax import lax
from jax.experimental import pallas as pl
from jax.experimental.pallas import tpu as pltpu
from jax.sharding import PartitionSpec as P

MESH = pl.DeviceIdType.MESH
HD = 128
ROWS = 256
NH = 3
WIDTH = NH * HD
D = 3072
NT = 8
NZ = 8
LOG2E = 1.4426950408889634
EXP_SCALE = LOG2E / (HD**0.5)
DEPTH = (4, 3)
FRESH = 2 * NZ
F32 = jnp.float32
BF16 = jnp.bfloat16


def dot(a, b):
    return jnp.dot(a, b, preferred_element_type=F32)


def kernel(
    tok_in, scale_in, shift_in, w_in, wo_in, sk_in, sv_in,
    out_ref,
    scale_ref, shift_ref, kv, vtmp, tok, mod, w, wo, wo2, att, att2, sum_out, sum_in, qown, qpart, qt, m_s, l_s, acc, sc_a, sc_b, mean_s, dev_s,
    osend, orecv, ssend, srecv,
    loc_sem, w_sem, ring_ss, ring_rs, d2d_ss, d2d_rs, tok_ss, tok_rs, att_ss, att_rs,
    q_ss, q_rs, o_ss, o_rs, st_ss, st_rs, wo_ss, wo_rs, w2_ss, w2_rs, wx_ss, wx_rs, sum_ss, sum_rs,
):
    p, t = lax.axis_index("patch"), lax.axis_index("tensor")
    b, z, c = lax.div(p, 16), lax.rem(lax.div(p, 2), NZ), lax.rem(p, 2)
    yh, x = lax.div(t, 4), lax.rem(t, 4)

    def dev(b=b, z=z, c=c, yh=yh, x=x):
        return (b * 16 + z * 2 + c, yh * 4 + x)

    def remote(src, dst, ss, rs, to):
        return pltpu.make_async_remote_copy(
            src_ref=src, dst_ref=dst, send_sem=ss, recv_sem=rs, device_id=to, device_id_type=MESH
        )

    dz = (1 - 2 * c, 2 * c - 1)
    zs = tuple(lax.rem(z + s + NZ, NZ) for s in dz)
    sibling, partner = dev(c=1 - c), dev(b=1 - b)
    xr, xl = dev(x=lax.rem(x + 1, 4)), dev(x=lax.rem(x + 3, 4))
    yo = dev(yh=1 - yh)
    me = z * 2 + c

    barrier = pltpu.get_barrier_semaphore()
    peers = [sibling, partner, dev(z=zs[0]), dev(z=zs[1])]
    for e in range(1, NT):
        peers.append((p, lax.rem(t + e, NT)))
    for peer in peers:
        pl.semaphore_signal(barrier, inc=1, device_id=peer, device_id_type=MESH)

    tok_load = pltpu.make_async_copy(tok_in, tok.at[t], loc_sem.at[0])
    k_loads, v_loads = [], []
    for h in range(NH):
        cols = pl.ds(h * HD, HD)
        k_loads.append(pltpu.make_async_copy(sk_in.at[:, cols], kv.at[me, h, 0], loc_sem.at[1 + 2 * h]))
        v_loads.append(pltpu.make_async_copy(sv_in.at[:, cols], vtmp.at[h], loc_sem.at[2 + 2 * h]))
    vec_loads = [
        pltpu.make_async_copy(scale_in, scale_ref, loc_sem.at[7]),
        pltpu.make_async_copy(shift_in, shift_ref, loc_sem.at[8]),
    ]
    w_loads = [pltpu.make_async_copy(w_in.at[j], w.at[j], w_sem.at[j]) for j in range(3)]
    for copy in [tok_load] + k_loads + v_loads + vec_loads + w_loads:
        copy.start()

    def put_values(slot, h, values):
        kv[slot, h, 1, :HD] = values[:HD].T
        kv[slot, h, 1, HD:] = values[HD:].T

    tok_load.wait()
    pl.semaphore_wait(barrier, len(peers))

    sent = []

    def go(make, *args):
        make(*args).start()
        sent.append((make, args))

    def drain():
        for make, args in sent:
            make(*args).wait_send()
        sent.clear()

    def slot_of(s, d):
        return lax.rem(z - d * dz[s] + NZ, NZ) * 2 + c

    def unit(slot, u):
        return kv.at[slot, u // 2, u % 2]

    def ring(s, u, d):
        view = unit(slot_of(s, d), u)
        return remote(view, view, ring_ss.at[s, u, d], ring_rs.at[s, u, d], dev(z=zs[s]))

    def share(k, u, slot):
        return remote(unit(slot, u), unit(slot, u), d2d_ss.at[k, u], d2d_rs.at[k, u], sibling)

    def own(u):
        if u % 2 == 0:
            k_loads[u // 2].wait()
        else:
            v_loads[u // 2].wait()
            put_values(me, u // 2, vtmp[u // 2])
        go(ring, 0, u, 0)
        go(ring, 1, u, 0)
        go(share, 0, u, me)

    def event(u, d):
        for s in (0, 1):
            if d > DEPTH[s]:
                continue
            slot = slot_of(s, d)
            remote(
                unit(slot, u), unit(slot, u), ring_ss.at[s, u, d - 1], ring_rs.at[s, u, d - 1], sibling
            ).wait_recv()
            if d < DEPTH[s]:
                go(ring, s, u, d)
            go(share, d + 4 * s, u, slot)

    slot_l, slot_r, slot_f = (yh * 4 + lax.rem(x + e, 4) for e in (3, 1, 2))
    slot_y, slot_yl, slot_yr, slot_yf = ((1 - yh) * 4 + lax.rem(x + e, 4) for e in (0, 3, 1, 2))
    L, R, Y, F, YL, YR, YF = range(0, 28, 4)

    def tok_copy(slot, q, to, kind):
        view = tok.at[slot, pl.ds(q * (ROWS // 4), ROWS // 4)]
        return remote(view, view, tok_ss.at[kind + q], tok_rs.at[kind + q], to)

    def tok_wait(slot, q, kind):
        tok_copy(slot, q, sibling, kind).wait_recv()

    def wo_cols(to):
        return pl.ds(pl.multiple_of(to * WIDTH, WIDTH), WIDTH)

    def wo_near(e, g):
        to = lax.rem(x + e, 4)
        src = wo_in.at[pl.ds(0, 2), c, :, wo_cols(g * 4 + to)]
        return remote(src, wo.at[x, g, :, c], wo_ss.at[2 * e + g], wo_rs.at[2 * e + g], dev(x=to))

    def wo_near_own(g):
        src = wo_in.at[pl.ds(0, 2), c, :, wo_cols(g * 4 + x)]
        return pltpu.make_async_copy(src, wo.at[x, g, :, c], wo_ss.at[g])

    def wo_all(e):
        to = yh * 4 + lax.rem(x + e, 4) if e < 4 else (1 - yh) * 4 + lax.rem(x + e, 4)
        src = wo_in.at[2, c, :, wo_cols(to)]
        return remote(src, wo2.at[t, c], w2_ss.at[e], w2_rs.at[e], (p, to))

    def wo_all_own():
        return pltpu.make_async_copy(wo_in.at[2, c, :, wo_cols(t)], wo2.at[t, c], w2_ss.at[0])

    def wo_share(half):
        return remote(wo.at[:, :, :, half], wo.at[:, :, :, half], wx_ss.at[0], wx_rs.at[0], sibling)

    def wo_share2(half):
        return remote(wo2.at[:, half], wo2.at[:, half], wx_ss.at[1], wx_rs.at[1], sibling)

    def wo_pass():
        for e in range(1, 4):
            for g in (0, 1):
                view = wo.at[lax.rem(x + 4 - e, 4), g, :, c]
                remote(view, view, wo_ss.at[2 * e + g], wo_rs.at[2 * e + g], sibling).wait_recv()
        for g in (0, 1):
            wo_near_own(g).wait()
        go(wo_share, c)

    def wo_pass2():
        for e in range(1, NT):
            frm = yh * 4 + lax.rem(x + 4 - e, 4) if e < 4 else (1 - yh) * 4 + lax.rem(x + 8 - e, 4)
            view = wo2.at[frm, c]
            remote(view, view, w2_ss.at[e], w2_rs.at[e], sibling).wait_recv()
        wo_all_own().wait()
        go(wo_share2, c)

    def stats(slot, seen):
        xb = tok[slot].astype(F32)
        mb = jnp.sum(xb, axis=1, keepdims=True) * (1.0 / WIDTH)
        cb = xb - mb
        sb = jnp.sum(cb * cb, axis=1, keepdims=True)
        if seen == 0:
            mean_s[...] = mb
            dev_s[...] = sb
        else:
            delta = mb - mean_s[...]
            mean_s[...] += delta * (1.0 / (seen + 1))
            dev_s[...] += sb + delta * delta * (WIDTH * seen / (seen + 1))

    def place(h, i):
        d, side = (i + 1) // 2, (i + 1) % 2
        chip = lax.rem(z - d * dz[side] + NZ, NZ)
        if d in (0, 4):
            k = d
        else:
            k = d if side else d + 4
        return k, chip * 2 + c, chip * 2 + 1 - c

    def block_wait(h, i, j):
        k, _, far = place(h, i)
        share(k, 2 * h + j, far).wait_recv()

    def scores(h, i, lo, hi, buf):
        _, near, far = place(h, i)
        query = qt[h, :, lo:hi]
        if i == 0:
            parts = []
            if lo == 0:
                parts.append(dot(kv[FRESH, h, 0], query[:, :ROWS]))
            if hi > ROWS:
                parts.append(dot(kv[near, h, 0], query[:, ROWS - lo :]))
            first = parts[0] if len(parts) == 1 else jnp.concatenate(parts, axis=1)
        else:
            first = dot(kv[near, h, 0], query)
        top = None
        for j, s in enumerate((first, dot(kv[far, h, 0], query))):
            s = s * EXP_SCALE
            buf[j, :, lo:hi] = s
            part = s.max(axis=0, keepdims=True)
            top = part if top is None else jnp.maximum(top, part)
        return top

    def values(slot, h):
        return jnp.concatenate([kv[slot, h, 1, :HD], kv[slot, h, 1, HD:]], axis=1)

    def weigh(h, i, lo, hi, buf, top):
        _, near, far = place(h, i)
        new = top if i == 0 else jnp.maximum(m_s[h, :, lo:hi], top)
        total, summed = None, None
        for j, slot in enumerate((near, far)):
            weights = jnp.exp2(buf[j, :, lo:hi] - new)
            part = jnp.sum(weights, axis=0, keepdims=True)
            weights = weights.astype(BF16)
            if i == 0 and j == 0:
                parts = []
                if lo == 0:
                    parts.append(dot(values(FRESH, h), weights[:, :ROWS]))
                if hi > ROWS:
                    parts.append(dot(values(slot, h), weights[:, ROWS - lo :]))
                prod = parts[0] if len(parts) == 1 else jnp.concatenate(parts, axis=1)
            else:
                prod = dot(values(slot, h), weights)
            total = part if total is None else total + part
            summed = prod if summed is None else summed + prod
        if i == 0:
            l_s[h, :, lo:hi] = total
            acc[h, :, lo:hi] = summed
        else:
            alpha = jnp.exp2(m_s[h, :, lo:hi] - new)
            l_s[h, :, lo:hi] = l_s[h, :, lo:hi] * alpha + total
            acc[h, :, lo:hi] = acc[h, :, lo:hi] * alpha + summed
        m_s[h, :, lo:hi] = new

    def o_copy(h):
        return remote(osend.at[h], orecv.at[h], o_ss.at[h], o_rs.at[h], partner)

    def s_copy(h):
        return remote(ssend.at[h], srecv.at[h], st_ss.at[h], st_rs.at[h], partner)

    def q_copy(h):
        return remote(qown.at[h], qpart.at[h], q_ss.at[h], q_rs.at[h], partner)

    def give(h):
        total = l_s[h, :, ROWS:]
        osend[h] = (acc[h, :, ROWS:] / total).astype(BF16)
        ssend[h, 0:1, :] = m_s[h, :, ROWS:]
        ssend[h, 1:2, :] = total
        go(o_copy, h)
        go(s_copy, h)

    half = (pl.ds(0, ROWS // 2), pl.ds(ROWS // 2, ROWS // 2))

    def att_copy(h, e):
        if h < 2:
            view, to = att.at[h, x], dev(x=lax.rem(x + e, 4))
        else:
            view, to = att2.at[t], dev(x=lax.rem(x + e, 4))
        return remote(view, view, att_ss.at[h, e], att_rs.at[h, e], to)

    def att_cross(r):
        view = att2.at[t, half[r]]
        return remote(view, view, att_ss.at[2, 4 + r], att_rs.at[2, 4 + r], yo)

    def att_pass(r, e):
        view, i = att2.at[slot_y, half[r]], 5 + 3 * r + e
        return remote(view, view, att_ss.at[2, i], att_rs.at[2, i], dev(x=lax.rem(x + e, 4)))

    def att_wait(h, e):
        view = att.at[h, lax.rem(x + 4 - e, 4)] if h < 2 else att2.at[yh * 4 + lax.rem(x + 4 - e, 4)]
        remote(view, view, att_ss.at[h, e], att_rs.at[h, e], sibling).wait_recv()

    def att_wait_cross(r):
        view = att2.at[slot_y, half[r]]
        remote(view, view, att_ss.at[2, 4 + r], att_rs.at[2, 4 + r], sibling).wait_recv()

    def att_wait_pass(r, e):
        view, i = att2.at[(1 - yh) * 4 + lax.rem(x + 4 - e, 4), half[r]], 5 + 3 * r + e
        remote(view, view, att_ss.at[2, i], att_rs.at[2, i], sibling).wait_recv()

    def merge(h):
        o_copy(h).wait_recv()
        s_copy(h).wait_recv()
        m1, m2 = m_s[h, :, :ROWS], srecv[h, 0:1, :]
        top = jnp.maximum(m1, m2)
        w1 = jnp.exp2(m1 - top)
        w2 = jnp.exp2(m2 - top) * srecv[h, 1:2, :]
        inv = 1.0 / (l_s[h, :, :ROWS] * w1 + w2)
        attended = acc[h, :, :ROWS] * (w1 * inv) + orecv[h].astype(F32) * (w2 * inv)
        attended = attended.T.astype(BF16)
        if h < 2:
            att[h, x] = attended
        else:
            att2[t] = attended
        if h == 2:
            go(att_cross, 0)
            go(att_cross, 1)
        for e in (1, 3, 2):
            go(att_copy, h, e)

    def project(g):
        total = None
        for s in range(4):
            lhs = jnp.concatenate([att[0, s], att[1, s]], axis=1)
            part = dot(lhs, wo[s, g].reshape(2 * HD, WIDTH))
            total = part if total is None else total + part
        return total

    def project_last():
        total = None
        for s in range(0, NT, 2):
            lhs = jnp.concatenate([att2[s], att2[s + 1]], axis=1)
            part = dot(lhs, wo2[pl.ds(s, 2)].reshape(2 * HD, WIDTH))
            total = part if total is None else total + part
        return total

    def sum_copy():
        return remote(sum_out, sum_in, sum_ss.at[0], sum_rs.at[0], yo)

    for q in (0, 1):
        go(tok_copy, t, q, xr, L)
        go(tok_copy, t, 3 - q, xl, R)
    for q in range(4):
        go(tok_copy, t, q, yo, Y)
    for u in range(4):
        own(u)
    stats(t, 0)
    for q in (0, 1):
        tok_wait(slot_l, q, L)
        go(tok_copy, slot_l, q, xr, F)
        tok_wait(slot_r, 3 - q, R)
        go(tok_copy, slot_r, 3 - q, xl, F)
    for q in (0, 1):
        go(tok_copy, t, 3 - q, xr, L)
        go(tok_copy, t, q, xl, R)
    event(0, 1)
    for q in range(4):
        tok_wait(slot_y, q, Y)
        go(tok_copy, slot_y, q, xr, YL)
        go(tok_copy, slot_y, q, xl, YR)
    event(1, 1)
    event(2, 1)
    for q in (0, 3, 1, 2):
        tok_wait(slot_f, q, F)
        go(tok_copy, slot_f, q, yo, YF)
    event(3, 1)
    own(4)
    own(5)
    for q in (0, 1):
        tok_wait(slot_l, 3 - q, L)
        tok_wait(slot_r, q, R)
    stats(slot_l, 1)
    stats(slot_r, 2)
    stats(slot_y, 3)
    stats(slot_f, 4)
    event(0, 2)
    event(1, 2)
    for q in range(4):
        tok_wait(slot_yl, q, YL)
        tok_wait(slot_yr, q, YR)
    stats(slot_yl, 5)
    stats(slot_yr, 6)
    event(2, 2)
    for q in (0, 3, 1, 2):
        tok_wait(slot_yf, q, YF)
    stats(slot_yf, 7)
    for g in (0, 1):
        wo_near_own(g).start()
        for e in (1, 2, 3):
            go(wo_near, e, g)
    wo_all_own().start()
    for e in (1, 2, 3):
        go(wo_all, e)
    for copy in vec_loads:
        copy.wait()
    mean = mean_s[...]
    inv = lax.rsqrt(dev_s[...] * (1.0 / D) + 1e-6)
    after = {0: [(3, 2)], 1: [(4, 1)], 2: [(5, 1)]}
    for j in range(3):
        w_loads[j].wait()
        if j == 0:
            res = None
            for i in range(NT):
                cols = slice(i * WIDTH, (i + 1) * WIDTH)
                normed = (tok[i].astype(F32) - mean) * inv
                slab = (normed * (1.0 + scale_ref[:, cols]) + shift_ref[:, cols]).astype(BF16)
                mod[:, cols] = slab
                part = dot(slab, w[0, cols])
                res = part if res is None else res + part
        else:
            res = dot(mod[...], w[j])
        res = res.astype(BF16)
        for h in range(NH):
            head = res[:, h * HD : (h + 1) * HD]
            if j == 0:
                qown[h] = head
                go(q_copy, h)
                qt[h, :, :ROWS] = head.T
            elif j == 1:
                kv[FRESH, h, 0] = head
            else:
                put_values(FRESH, h, head)
        for u, d in after[j]:
            event(u, d)
    for e in (4, 5, 6, 7):
        go(wo_all, e)

    def query_in(h):
        q_copy(h).wait_recv()
        qt[h, :, ROWS:] = qpart[h].T

    order = [(0, i, 0, ROWS) for i in range(5)] + [(0, i, ROWS, 2 * ROWS) for i in range(5)]
    rest = [(1, i) for i in range(5)] + [(2, 0), (2, 1), (2, 2)]
    rest += [(0, 5), (0, 6), (1, 5), (1, 6), (0, 7), (1, 7)] + [(2, i) for i in range(3, 8)]
    order += [(h, i, 0, 2 * ROWS) for h, i in rest]
    due = {
        (0, 0, 0): [lambda: event(0, 3)],
        (0, 0, ROWS): [lambda: query_in(0), lambda: event(1, 3)],
        (1, 0, 0): [lambda: query_in(1)],
        (1, 1, 0): [lambda: event(2, 3)],
        (1, 3, 0): [lambda: event(3, 3)],
        (1, 4, 0): [lambda: event(4, 2)],
        (2, 0, 0): [lambda: query_in(2)],
        (2, 2, 0): [lambda: event(5, 2)],
        (0, 6, 0): [lambda: event(0, 4)],
        (1, 5, 0): [lambda: event(1, 4)],
        (1, 6, 0): [lambda: event(2, 4)],
        (0, 7, 0): [lambda: event(3, 4), lambda: event(4, 3)],
        (2, 3, 0): [lambda: give(0), lambda: event(5, 3)],
        (2, 4, 0): [lambda: give(1), wo_pass],
        (2, 5, 0): [wo_pass2],
        (2, 6, 0): [lambda: event(4, 4)],
        (2, 7, 0): [lambda: event(5, 4), lambda: merge(0), lambda: merge(1)],
    }
    groups = [0, 5, 10, 12, 14, 16, 18, 20] + list(range(21, len(order) + 1))
    bufs = (sc_a, sc_b)
    waited = set()

    def ready(n, j):
        h, i, lo, _ = order[n]
        if j == 0:
            for f in due.get((h, i, lo), ()):
                f()
        if (h, i, j) not in waited:
            waited.add((h, i, j))
            block_wait(h, i, j)

    fresh_start = (0, 5)
    for start, stop in zip(groups, groups[1:]):
        last = stop if stop in fresh_start or stop == len(order) else stop + 1
        for n in range(start if start in fresh_start else start + 1, last):
            ready(n, 0)
        for n in range(start, stop):
            ready(n, 1)
        if start in fresh_start:
            top = scores(*order[start], bufs[start % 2])
        for n in range(start, stop):
            if n + 1 < last:
                later = scores(*order[n + 1], bufs[(n + 1) % 2])
            weigh(*order[n], bufs[n % 2], top)
            top = later
    give(2)
    wo_share(1 - c).wait_recv()
    merge(2)
    for h in (0, 1):
        for e in (1, 2, 3):
            att_wait(h, e)
    sum_out[...] = project(1 - yh).astype(BF16)
    go(sum_copy)
    out_ref[...] = project(yh)
    for r in (0, 1):
        att_wait_cross(r)
        for e in (1, 3, 2):
            go(att_pass, r, e)
    for e in (1, 2, 3):
        att_wait(2, e)
    wo_share2(1 - c).wait_recv()
    sum_copy().wait_recv()
    out_ref[...] += sum_in[...].astype(F32)
    drain()
    for r in (0, 1):
        for e in (1, 2, 3):
            att_wait_pass(r, e)
    out_ref[...] += project_last()


def block(tokens, scale, shift, w, wo, sk, sv):
    dma, vmem = pltpu.SemaphoreType.DMA, pltpu.VMEM
    anywhere = pl.BlockSpec(memory_space=pl.ANY)
    inside = pl.BlockSpec(memory_space=pltpu.VMEM)
    return pl.pallas_call(
        kernel,
        out_shape=jax.ShapeDtypeStruct((ROWS, WIDTH), F32),
        in_specs=[anywhere] * 7,
        out_specs=inside,
        scratch_shapes=[
            vmem((1, D), F32),
            vmem((1, D), F32),
            vmem((2 * NZ + 1, NH, 2, ROWS, HD), BF16),
            vmem((NH, ROWS, HD), BF16),
            vmem((NT, ROWS, WIDTH), BF16),
            vmem((ROWS, D), BF16),
            vmem((3, D, WIDTH), BF16),
            vmem((4, 2, 2, 2, 64, WIDTH), BF16),
            vmem((NT, 2, 64, WIDTH), BF16),
            vmem((2, 4, ROWS, HD), BF16),
            vmem((NT, ROWS, HD), BF16),
            vmem((ROWS, WIDTH), BF16),
            vmem((ROWS, WIDTH), BF16),
            vmem((NH, ROWS, HD), BF16),
            vmem((NH, ROWS, HD), BF16),
            vmem((NH, HD, 2 * ROWS), BF16),
            vmem((NH, 1, 2 * ROWS), F32),
            vmem((NH, 1, 2 * ROWS), F32),
            vmem((NH, HD, 2 * ROWS), F32),
            vmem((2, ROWS, 2 * ROWS), F32),
            vmem((2, ROWS, 2 * ROWS), F32),
            vmem((ROWS, 1), F32),
            vmem((ROWS, 1), F32),
            vmem((NH, HD, ROWS), BF16),
            vmem((NH, HD, ROWS), BF16),
            vmem((NH, 8, ROWS), F32),
            vmem((NH, 8, ROWS), F32),
            dma((9,)),
            dma((3,)),
            dma((2, 2 * NH, 4)),
            dma((2, 2 * NH, 4)),
            dma((8, 2 * NH)),
            dma((8, 2 * NH)),
            dma((28,)),
            dma((28,)),
            dma((NH, 12)),
            dma((NH, 12)),
            dma((NH,)),
            dma((NH,)),
            dma((NH,)),
            dma((NH,)),
            dma((NH,)),
            dma((NH,)),
            dma((NT,)),
            dma((NT,)),
            dma((NT,)),
            dma((NT,)),
            dma((2,)),
            dma((2,)),
            dma((1,)),
            dma((1,)),
        ],
        compiler_params=pltpu.CompilerParams(
            collective_id=0, has_side_effects=True, vmem_limit_bytes=56 * 1024 * 1024
        ),
        name="attention_block",
    )(tokens, scale, shift, w, wo, sk, sv)


def local(tokens, shift, scale, gate, w_qkv, w_out, stale_keys, stale_values):
    summed = block(
        tokens,
        scale.reshape(1, D),
        shift.reshape(1, D),
        jnp.transpose(w_qkv, (1, 0, 2)),
        w_out.reshape(NH, 2, 64, D),
        stale_keys,
        stale_values,
    )
    branch = gate * summed
    return ((tokens.astype(F32) + branch).astype(BF16), branch)


def solution(mesh):
    in_specs = (
        P("patch", "tensor"),
        P(),
        P(),
        P("tensor"),
        P(None, None, "tensor"),
        P("tensor", None),
        P("patch", "tensor"),
        P("patch", "tensor"),
    )
    out_specs = (P("patch", "tensor"), P("patch", "tensor"))
    return jax.shard_map(local, mesh=mesh, in_specs=in_specs, out_specs=out_specs, check_vma=False)
```

```python
import jax
import jax.numpy as jnp
from jax import lax
from jax.experimental import pallas as pl
from jax.experimental.pallas import tpu as pltpu
from jax.sharding import PartitionSpec as P

MESH = pl.DeviceIdType.MESH
HD = 128
ROWS = 256
NH = 3
WIDTH = NH * HD
D = 3072
NT = 8
NZ = 8
LOG2E = 1.4426950408889634
EXP_SCALE = LOG2E / (HD**0.5)
DEPTH = (4, 3)
FRESH = 2 * NZ
F32 = jnp.float32
BF16 = jnp.bfloat16


def dot(a, b):
    return jnp.dot(a, b, preferred_element_type=F32)


def kernel(
    tok_in, scale_in, shift_in, w_in, wo_in, sk_in, sv_in,
    out_ref,
    scale_ref, shift_ref, kv, vtmp, tok, mod, w, wo, wo2, att, att2, sum_out, sum_in, qown, qpart, qt, m_s, l_s, acc, sc_a, sc_b, mean_s, dev_s,
    osend, orecv, ssend, srecv,
    loc_sem, w_sem, ring_ss, ring_rs, d2d_ss, d2d_rs, tok_ss, tok_rs, att_ss, att_rs,
    q_ss, q_rs, o_ss, o_rs, st_ss, st_rs, wo_ss, wo_rs, w2_ss, w2_rs, wx_ss, wx_rs, sum_ss, sum_rs,
):
    p, t = lax.axis_index("patch"), lax.axis_index("tensor")
    b, z, c = lax.div(p, 16), lax.rem(lax.div(p, 2), NZ), lax.rem(p, 2)
    yh, x = lax.div(t, 4), lax.rem(t, 4)

    def dev(b=b, z=z, c=c, yh=yh, x=x):
        return (b * 16 + z * 2 + c, yh * 4 + x)

    def remote(src, dst, ss, rs, to):
        return pltpu.make_async_remote_copy(
            src_ref=src, dst_ref=dst, send_sem=ss, recv_sem=rs, device_id=to, device_id_type=MESH
        )

    dz = (1 - 2 * c, 2 * c - 1)
    zs = tuple(lax.rem(z + s + NZ, NZ) for s in dz)
    sibling, partner = dev(c=1 - c), dev(b=1 - b)
    xr, xl = dev(x=lax.rem(x + 1, 4)), dev(x=lax.rem(x + 3, 4))
    yo = dev(yh=1 - yh)
    me = z * 2 + c

    barrier = pltpu.get_barrier_semaphore()
    peers = [sibling, partner, dev(z=zs[0]), dev(z=zs[1])]
    for e in range(1, NT):
        peers.append((p, lax.rem(t + e, NT)))
    for peer in peers:
        pl.semaphore_signal(barrier, inc=1, device_id=peer, device_id_type=MESH)

    tok_load = pltpu.make_async_copy(tok_in, tok.at[t], loc_sem.at[0])
    k_loads, v_loads = [], []
    for h in range(NH):
        cols = pl.ds(h * HD, HD)
        k_loads.append(pltpu.make_async_copy(sk_in.at[:, cols], kv.at[me, h, 0], loc_sem.at[1 + 2 * h]))
        v_loads.append(pltpu.make_async_copy(sv_in.at[:, cols], vtmp.at[h], loc_sem.at[2 + 2 * h]))
    vec_loads = [
        pltpu.make_async_copy(scale_in, scale_ref, loc_sem.at[7]),
        pltpu.make_async_copy(shift_in, shift_ref, loc_sem.at[8]),
    ]
    w_loads = [pltpu.make_async_copy(w_in.at[j], w.at[j], w_sem.at[j]) for j in range(3)]
    for copy in [tok_load] + k_loads + v_loads + vec_loads + w_loads:
        copy.start()

    def put_values(slot, h, values):
        kv[slot, h, 1, :HD] = values[:HD].T
        kv[slot, h, 1, HD:] = values[HD:].T

    tok_load.wait()
    pl.semaphore_wait(barrier, len(peers))

    sent = []

    def go(make, *args):
        make(*args).start()
        sent.append((make, args))

    def drain():
        for make, args in sent:
            make(*args).wait_send()
        sent.clear()

    def slot_of(s, d):
        return lax.rem(z - d * dz[s] + NZ, NZ) * 2 + c

    def unit(slot, u):
        return kv.at[slot, u // 2, u % 2]

    def ring(s, u, d):
        view = unit(slot_of(s, d), u)
        return remote(view, view, ring_ss.at[s, u, d], ring_rs.at[s, u, d], dev(z=zs[s]))

    def share(k, u, slot):
        return remote(unit(slot, u), unit(slot, u), d2d_ss.at[k, u], d2d_rs.at[k, u], sibling)

    def own(u):
        if u % 2 == 0:
            k_loads[u // 2].wait()
        else:
            v_loads[u // 2].wait()
            put_values(me, u // 2, vtmp[u // 2])
        go(ring, 0, u, 0)
        go(ring, 1, u, 0)
        go(share, 0, u, me)

    def event(u, d):
        for s in (0, 1):
            if d > DEPTH[s]:
                continue
            slot = slot_of(s, d)
            remote(
                unit(slot, u), unit(slot, u), ring_ss.at[s, u, d - 1], ring_rs.at[s, u, d - 1], sibling
            ).wait_recv()
            if d < DEPTH[s]:
                go(ring, s, u, d)
            go(share, d + 4 * s, u, slot)

    slot_l, slot_r, slot_f = (yh * 4 + lax.rem(x + e, 4) for e in (3, 1, 2))
    slot_y, slot_yl, slot_yr, slot_yf = ((1 - yh) * 4 + lax.rem(x + e, 4) for e in (0, 3, 1, 2))
    L, R, Y, F, YL, YR, YF = range(0, 28, 4)

    def tok_copy(slot, q, to, kind):
        view = tok.at[slot, pl.ds(q * (ROWS // 4), ROWS // 4)]
        return remote(view, view, tok_ss.at[kind + q], tok_rs.at[kind + q], to)

    def tok_wait(slot, q, kind):
        tok_copy(slot, q, sibling, kind).wait_recv()

    def wo_cols(to):
        return pl.ds(pl.multiple_of(to * WIDTH, WIDTH), WIDTH)

    def wo_near(e, g):
        to = lax.rem(x + e, 4)
        src = wo_in.at[pl.ds(0, 2), c, :, wo_cols(g * 4 + to)]
        return remote(src, wo.at[x, g, :, c], wo_ss.at[2 * e + g], wo_rs.at[2 * e + g], dev(x=to))

    def wo_near_own(g):
        src = wo_in.at[pl.ds(0, 2), c, :, wo_cols(g * 4 + x)]
        return pltpu.make_async_copy(src, wo.at[x, g, :, c], wo_ss.at[g])

    def wo_all(e):
        to = yh * 4 + lax.rem(x + e, 4) if e < 4 else (1 - yh) * 4 + lax.rem(x + e, 4)
        src = wo_in.at[2, c, :, wo_cols(to)]
        return remote(src, wo2.at[t, c], w2_ss.at[e], w2_rs.at[e], (p, to))

    def wo_all_own():
        return pltpu.make_async_copy(wo_in.at[2, c, :, wo_cols(t)], wo2.at[t, c], w2_ss.at[0])

    def wo_share(half):
        return remote(wo.at[:, :, :, half], wo.at[:, :, :, half], wx_ss.at[0], wx_rs.at[0], sibling)

    def wo_share2(half):
        return remote(wo2.at[:, half], wo2.at[:, half], wx_ss.at[1], wx_rs.at[1], sibling)

    def wo_pass():
        for e in range(1, 4):
            for g in (0, 1):
                view = wo.at[lax.rem(x + 4 - e, 4), g, :, c]
                remote(view, view, wo_ss.at[2 * e + g], wo_rs.at[2 * e + g], sibling).wait_recv()
        for g in (0, 1):
            wo_near_own(g).wait()
        go(wo_share, c)

    def wo_pass2():
        for e in range(1, NT):
            frm = yh * 4 + lax.rem(x + 4 - e, 4) if e < 4 else (1 - yh) * 4 + lax.rem(x + 8 - e, 4)
            view = wo2.at[frm, c]
            remote(view, view, w2_ss.at[e], w2_rs.at[e], sibling).wait_recv()
        wo_all_own().wait()
        go(wo_share2, c)

    def stats(slot, seen):
        xb = tok[slot].astype(F32)
        mb = jnp.sum(xb, axis=1, keepdims=True) * (1.0 / WIDTH)
        cb = xb - mb
        sb = jnp.sum(cb * cb, axis=1, keepdims=True)
        if seen == 0:
            mean_s[...] = mb
            dev_s[...] = sb
        else:
            delta = mb - mean_s[...]
            mean_s[...] += delta * (1.0 / (seen + 1))
            dev_s[...] += sb + delta * delta * (WIDTH * seen / (seen + 1))

    def place(h, i):
        d, side = (i + 1) // 2, (i + 1) % 2
        chip = lax.rem(z - d * dz[side] + NZ, NZ)
        if d in (0, 4):
            k = d
        else:
            k = d if side else d + 4
        return k, chip * 2 + c, chip * 2 + 1 - c

    def block_wait(h, i, j):
        k, _, far = place(h, i)
        share(k, 2 * h + j, far).wait_recv()

    def scores(h, i, lo, hi, buf):
        _, near, far = place(h, i)
        query = qt[h, :, lo:hi]
        if i == 0:
            parts = []
            if lo == 0:
                parts.append(dot(kv[FRESH, h, 0], query[:, :ROWS]))
            if hi > ROWS:
                parts.append(dot(kv[near, h, 0], query[:, ROWS - lo :]))
            first = parts[0] if len(parts) == 1 else jnp.concatenate(parts, axis=1)
        else:
            first = dot(kv[near, h, 0], query)
        top = None
        for j, s in enumerate((first, dot(kv[far, h, 0], query))):
            s = s * EXP_SCALE
            buf[j, :, lo:hi] = s
            part = s.max(axis=0, keepdims=True)
            top = part if top is None else jnp.maximum(top, part)
        return top

    def values(slot, h):
        return jnp.concatenate([kv[slot, h, 1, :HD], kv[slot, h, 1, HD:]], axis=1)

    def weigh(h, i, lo, hi, buf, top):
        _, near, far = place(h, i)
        new = top if i == 0 else jnp.maximum(m_s[h, :, lo:hi], top)
        total, summed = None, None
        for j, slot in enumerate((near, far)):
            weights = jnp.exp2(buf[j, :, lo:hi] - new)
            part = jnp.sum(weights, axis=0, keepdims=True)
            weights = weights.astype(BF16)
            if i == 0 and j == 0:
                parts = []
                if lo == 0:
                    parts.append(dot(values(FRESH, h), weights[:, :ROWS]))
                if hi > ROWS:
                    parts.append(dot(values(slot, h), weights[:, ROWS - lo :]))
                prod = parts[0] if len(parts) == 1 else jnp.concatenate(parts, axis=1)
            else:
                prod = dot(values(slot, h), weights)
            total = part if total is None else total + part
            summed = prod if summed is None else summed + prod
        if i == 0:
            l_s[h, :, lo:hi] = total
            acc[h, :, lo:hi] = summed
        else:
            alpha = jnp.exp2(m_s[h, :, lo:hi] - new)
            l_s[h, :, lo:hi] = l_s[h, :, lo:hi] * alpha + total
            acc[h, :, lo:hi] = acc[h, :, lo:hi] * alpha + summed
        m_s[h, :, lo:hi] = new

    def o_copy(h):
        return remote(osend.at[h], orecv.at[h], o_ss.at[h], o_rs.at[h], partner)

    def s_copy(h):
        return remote(ssend.at[h], srecv.at[h], st_ss.at[h], st_rs.at[h], partner)

    def q_copy(h):
        return remote(qown.at[h], qpart.at[h], q_ss.at[h], q_rs.at[h], partner)

    def give(h):
        total = l_s[h, :, ROWS:]
        osend[h] = (acc[h, :, ROWS:] / total).astype(BF16)
        ssend[h, 0:1, :] = m_s[h, :, ROWS:]
        ssend[h, 1:2, :] = total
        go(o_copy, h)
        go(s_copy, h)

    half = (pl.ds(0, ROWS // 2), pl.ds(ROWS // 2, ROWS // 2))

    def att_copy(h, e):
        if h < 2:
            view, to = att.at[h, x], dev(x=lax.rem(x + e, 4))
        else:
            view, to = att2.at[t], dev(x=lax.rem(x + e, 4))
        return remote(view, view, att_ss.at[h, e], att_rs.at[h, e], to)

    def att_cross(r):
        view = att2.at[t, half[r]]
        return remote(view, view, att_ss.at[2, 4 + r], att_rs.at[2, 4 + r], yo)

    def att_pass(r, e):
        view, i = att2.at[slot_y, half[r]], 5 + 3 * r + e
        return remote(view, view, att_ss.at[2, i], att_rs.at[2, i], dev(x=lax.rem(x + e, 4)))

    def att_wait(h, e):
        view = att.at[h, lax.rem(x + 4 - e, 4)] if h < 2 else att2.at[yh * 4 + lax.rem(x + 4 - e, 4)]
        remote(view, view, att_ss.at[h, e], att_rs.at[h, e], sibling).wait_recv()

    def att_wait_cross(r):
        view = att2.at[slot_y, half[r]]
        remote(view, view, att_ss.at[2, 4 + r], att_rs.at[2, 4 + r], sibling).wait_recv()

    def att_wait_pass(r, e):
        view, i = att2.at[(1 - yh) * 4 + lax.rem(x + 4 - e, 4), half[r]], 5 + 3 * r + e
        remote(view, view, att_ss.at[2, i], att_rs.at[2, i], sibling).wait_recv()

    def merge(h):
        o_copy(h).wait_recv()
        s_copy(h).wait_recv()
        m1, m2 = m_s[h, :, :ROWS], srecv[h, 0:1, :]
        top = jnp.maximum(m1, m2)
        w1 = jnp.exp2(m1 - top)
        w2 = jnp.exp2(m2 - top) * srecv[h, 1:2, :]
        inv = 1.0 / (l_s[h, :, :ROWS] * w1 + w2)
        attended = acc[h, :, :ROWS] * (w1 * inv) + orecv[h].astype(F32) * (w2 * inv)
        attended = attended.T.astype(BF16)
        if h < 2:
            att[h, x] = attended
        else:
            att2[t] = attended
        if h == 2:
            go(att_cross, 0)
            go(att_cross, 1)
        for e in (1, 3, 2):
            go(att_copy, h, e)

    def project(g):
        total = None
        for s in range(4):
            lhs = jnp.concatenate([att[0, s], att[1, s]], axis=1)
            part = dot(lhs, wo[s, g].reshape(2 * HD, WIDTH))
            total = part if total is None else total + part
        return total

    def project_last():
        total = None
        for s in range(0, NT, 2):
            lhs = jnp.concatenate([att2[s], att2[s + 1]], axis=1)
            part = dot(lhs, wo2[pl.ds(s, 2)].reshape(2 * HD, WIDTH))
            total = part if total is None else total + part
        return total

    def sum_copy():
        return remote(sum_out, sum_in, sum_ss.at[0], sum_rs.at[0], yo)

    for q in (0, 1):
        go(tok_copy, t, q, xr, L)
        go(tok_copy, t, 3 - q, xl, R)
    for q in range(4):
        go(tok_copy, t, q, yo, Y)
    for u in range(4):
        own(u)
    stats(t, 0)
    for q in (0, 1):
        tok_wait(slot_l, q, L)
        go(tok_copy, slot_l, q, xr, F)
        tok_wait(slot_r, 3 - q, R)
        go(tok_copy, slot_r, 3 - q, xl, F)
    for q in (0, 1):
        go(tok_copy, t, 3 - q, xr, L)
        go(tok_copy, t, q, xl, R)
    event(0, 1)
    for q in range(4):
        tok_wait(slot_y, q, Y)
        go(tok_copy, slot_y, q, xr, YL)
        go(tok_copy, slot_y, q, xl, YR)
    event(1, 1)
    event(2, 1)
    for q in (0, 3, 1, 2):
        tok_wait(slot_f, q, F)
        go(tok_copy, slot_f, q, yo, YF)
    event(3, 1)
    own(4)
    own(5)
    for q in (0, 1):
        tok_wait(slot_l, 3 - q, L)
        tok_wait(slot_r, q, R)
    stats(slot_l, 1)
    stats(slot_r, 2)
    stats(slot_y, 3)
    stats(slot_f, 4)
    event(0, 2)
    event(1, 2)
    for q in range(4):
        tok_wait(slot_yl, q, YL)
        tok_wait(slot_yr, q, YR)
    stats(slot_yl, 5)
    stats(slot_yr, 6)
    event(2, 2)
    for q in (0, 3, 1, 2):
        tok_wait(slot_yf, q, YF)
    stats(slot_yf, 7)
    for g in (0, 1):
        wo_near_own(g).start()
        for e in (1, 2, 3):
            go(wo_near, e, g)
    wo_all_own().start()
    for e in (1, 2, 3):
        go(wo_all, e)
    for copy in vec_loads:
        copy.wait()
    mean = mean_s[...]
    inv = lax.rsqrt(dev_s[...] * (1.0 / D) + 1e-6)
    after = {0: [(3, 2)], 1: [(4, 1)], 2: [(5, 1)]}
    for j in range(3):
        w_loads[j].wait()
        if j == 0:
            res = None
            for i in range(NT):
                cols = slice(i * WIDTH, (i + 1) * WIDTH)
                normed = (tok[i].astype(F32) - mean) * inv
                slab = (normed * (1.0 + scale_ref[:, cols]) + shift_ref[:, cols]).astype(BF16)
                mod[:, cols] = slab
                part = dot(slab, w[0, cols])
                res = part if res is None else res + part
        else:
            res = dot(mod[...], w[j])
        res = res.astype(BF16)
        for h in range(NH):
            head = res[:, h * HD : (h + 1) * HD]
            if j == 0:
                qown[h] = head
                go(q_copy, h)
                qt[h, :, :ROWS] = head.T
            elif j == 1:
                kv[FRESH, h, 0] = head
            else:
                put_values(FRESH, h, head)
        for u, d in after[j]:
            event(u, d)
    for e in (4, 5, 6, 7):
        go(wo_all, e)

    def query_in(h):
        q_copy(h).wait_recv()
        qt[h, :, ROWS:] = qpart[h].T

    order = [(0, i, 0, ROWS) for i in range(5)] + [(0, i, ROWS, 2 * ROWS) for i in range(5)]
    rest = [(1, i) for i in range(5)] + [(2, 0), (2, 1), (2, 2)]
    rest += [(0, 5), (0, 6), (1, 5), (1, 6), (0, 7), (1, 7)] + [(2, i) for i in range(3, 8)]
    order += [(h, i, 0, 2 * ROWS) for h, i in rest]
    due = {
        (0, 0, 0): [lambda: event(0, 3)],
        (0, 0, ROWS): [lambda: query_in(0), lambda: event(1, 3)],
        (1, 0, 0): [lambda: query_in(1), lambda: event(2, 3)],
        (1, 2, 0): [lambda: event(3, 3)],
        (1, 4, 0): [lambda: event(4, 2)],
        (2, 0, 0): [lambda: query_in(2)],
        (2, 2, 0): [lambda: event(5, 2)],
        (0, 6, 0): [lambda: event(0, 4)],
        (1, 5, 0): [lambda: event(1, 4)],
        (1, 6, 0): [lambda: event(2, 4)],
        (0, 7, 0): [lambda: event(3, 4), lambda: event(4, 3)],
        (2, 3, 0): [lambda: event(5, 3), lambda: give(0)],
        (2, 4, 0): [lambda: give(1)],
        (2, 6, 0): [lambda: event(4, 4)],
        (2, 7, 0): [lambda: event(5, 4), lambda: merge(0), lambda: merge(1), wo_pass, wo_pass2],
    }
    groups = [0, 5, 10, 12, 14, 16, 18, 20] + list(range(21, len(order) + 1))
    bufs = (sc_a, sc_b)
    waited = set()

    def ready(n, j):
        h, i, lo, _ = order[n]
        if j == 0:
            for f in due.get((h, i, lo), ()):
                f()
        if (h, i, j) not in waited:
            waited.add((h, i, j))
            block_wait(h, i, j)

    fresh_start = (0, 5)
    for start, stop in zip(groups, groups[1:]):
        last = stop if stop in fresh_start or stop == len(order) else stop + 1
        for n in range(start if start in fresh_start else start + 1, last):
            ready(n, 0)
        for n in range(start, stop):
            ready(n, 1)
        if start in fresh_start:
            top = scores(*order[start], bufs[start % 2])
        for n in range(start, stop):
            if n + 1 < last:
                later = scores(*order[n + 1], bufs[(n + 1) % 2])
            weigh(*order[n], bufs[n % 2], top)
            top = later
    give(2)
    wo_share(1 - c).wait_recv()
    merge(2)
    for h in (0, 1):
        for e in (1, 2, 3):
            att_wait(h, e)
    sum_out[...] = project(1 - yh).astype(BF16)
    go(sum_copy)
    out_ref[...] = project(yh)
    for r in (0, 1):
        att_wait_cross(r)
        for e in (1, 3, 2):
            go(att_pass, r, e)
    for e in (1, 2, 3):
        att_wait(2, e)
    wo_share2(1 - c).wait_recv()
    sum_copy().wait_recv()
    out_ref[...] += sum_in[...].astype(F32)
    drain()
    for r in (0, 1):
        for e in (1, 2, 3):
            att_wait_pass(r, e)
    out_ref[...] += project_last()


def block(tokens, scale, shift, w, wo, sk, sv):
    dma, vmem = pltpu.SemaphoreType.DMA, pltpu.VMEM
    anywhere = pl.BlockSpec(memory_space=pl.ANY)
    inside = pl.BlockSpec(memory_space=pltpu.VMEM)
    return pl.pallas_call(
        kernel,
        out_shape=jax.ShapeDtypeStruct((ROWS, WIDTH), F32),
        in_specs=[anywhere] * 7,
        out_specs=inside,
        scratch_shapes=[
            vmem((1, D), F32),
            vmem((1, D), F32),
            vmem((2 * NZ + 1, NH, 2, ROWS, HD), BF16),
            vmem((NH, ROWS, HD), BF16),
            vmem((NT, ROWS, WIDTH), BF16),
            vmem((ROWS, D), BF16),
            vmem((3, D, WIDTH), BF16),
            vmem((4, 2, 2, 2, 64, WIDTH), BF16),
            vmem((NT, 2, 64, WIDTH), BF16),
            vmem((2, 4, ROWS, HD), BF16),
            vmem((NT, ROWS, HD), BF16),
            vmem((ROWS, WIDTH), BF16),
            vmem((ROWS, WIDTH), BF16),
            vmem((NH, ROWS, HD), BF16),
            vmem((NH, ROWS, HD), BF16),
            vmem((NH, HD, 2 * ROWS), BF16),
            vmem((NH, 1, 2 * ROWS), F32),
            vmem((NH, 1, 2 * ROWS), F32),
            vmem((NH, HD, 2 * ROWS), F32),
            vmem((2, ROWS, 2 * ROWS), F32),
            vmem((2, ROWS, 2 * ROWS), F32),
            vmem((ROWS, 1), F32),
            vmem((ROWS, 1), F32),
            vmem((NH, HD, ROWS), BF16),
            vmem((NH, HD, ROWS), BF16),
            vmem((NH, 8, ROWS), F32),
            vmem((NH, 8, ROWS), F32),
            dma((9,)),
            dma((3,)),
            dma((2, 2 * NH, 4)),
            dma((2, 2 * NH, 4)),
            dma((8, 2 * NH)),
            dma((8, 2 * NH)),
            dma((28,)),
            dma((28,)),
            dma((NH, 12)),
            dma((NH, 12)),
            dma((NH,)),
            dma((NH,)),
            dma((NH,)),
            dma((NH,)),
            dma((NH,)),
            dma((NH,)),
            dma((NT,)),
            dma((NT,)),
            dma((NT,)),
            dma((NT,)),
            dma((2,)),
            dma((2,)),
            dma((1,)),
            dma((1,)),
        ],
        compiler_params=pltpu.CompilerParams(
            collective_id=0, has_side_effects=True, vmem_limit_bytes=56 * 1024 * 1024
        ),
        name="attention_block",
    )(tokens, scale, shift, w, wo, sk, sv)


def local(tokens, shift, scale, gate, w_qkv, w_out, stale_keys, stale_values):
    summed = block(
        tokens,
        scale.reshape(1, D),
        shift.reshape(1, D),
        jnp.transpose(w_qkv, (1, 0, 2)),
        w_out.reshape(NH, 2, 64, D),
        stale_keys,
        stale_values,
    )
    branch = gate * summed
    return ((tokens.astype(F32) + branch).astype(BF16), branch)


def solution(mesh):
    in_specs = (
        P("patch", "tensor"),
        P(),
        P(),
        P("tensor"),
        P(None, None, "tensor"),
        P("tensor", None),
        P("patch", "tensor"),
        P("patch", "tensor"),
    )
    out_specs = (P("patch", "tensor"), P("patch", "tensor"))
    return jax.shard_map(local, mesh=mesh, in_specs=in_specs, out_specs=out_specs, check_vma=False)
```
